512 devices in a mesh: user: 32 (over x, y), item: 16 (over z, core).
Axes of the slice: x: 4, y: 8, z: 8, core: 2. Of those that a mesh axis runs over, the one named last changes fastest.
Arguments:
- user_emb: bfloat16 [32768, 256], P(('user', 'item')), may hold values from -109 to 109
- item_codes: int32 [3, 32768], P(None, ('item', 'user')), may hold values from 0 to 255
- targets: int32 [32768], P(('user', 'item')), may hold values from 0 to 32767
- codebook: bfloat16 [3, 256, 256], replicated, may hold values from -6 to 6
Outputs:
- grad_user: float32 [32768, 256], P(('user', 'item'))
- grad_codebook: float32 [3, 256, 256], replicated
- loss: float32 [], replicated
The draws below stay inside these ranges and needn't reach their ends.
All inputs are finite; a program needn't handle non-finite values.
Results may differ from the reference program's by a relative error of at most 0.0015.
The reference program's roundings to bfloat16 on the way (of `item_vec` and `dlogits`) count: a program that leaves them out, or rounds other values in their place, can miss the bound.
Values may be sent and summed in bfloat16 or wider, within the bound.
A program may use at most 64 MiB of HBM per device.

```python
import jax
import jax.numpy as jnp
from jax import lax

D = 256
K = 256
LEVELS = 3
USER_BLK = 1024
USERS = 32768
ITEMS = 32768
N_USER = 32


def draw_user_emb(key, part):
    key = jax.random.fold_in(key, 11)
    values = jnp.clip(jax.random.normal(key, (USERS, D), jnp.float32), -6.0, 6.0)
    return values.astype(jnp.bfloat16)


def place_ends(entries, rng, least, largest):
    longest = entries.shape.index(max(entries.shape))
    spots = []
    for shift in (0, 1):
        where = [jax.random.randint(jax.random.fold_in(rng, axis), (), 0, length) for axis, length in enumerate(entries.shape)]
        where[longest] = (where[longest] + shift) % entries.shape[longest]
        spots.append(tuple(where))
    return entries.at[spots[0]].set(least).at[spots[1]].set(largest)


def normal_values(stream_key, extent, scale, reach, held_as=jnp.bfloat16):
    return jnp.clip(scale * jax.random.normal(stream_key, extent, jnp.float32), -reach, reach).astype(held_as)


def setup_inputs(seed: int = 0) -> dict:
    streams_of = jax.random.split(jax.random.key(seed), 5)
    return {
        "user_emb": draw_user_emb(jax.random.fold_in(streams_of[4], 71), 0),
        "item_codes": place_ends(jax.random.randint(streams_of[1], (LEVELS, ITEMS), 0, K), jax.random.fold_in(streams_of[1], 1), 0, K - 1).astype(jnp.int32),
        "targets": place_ends(jax.random.randint(streams_of[2], (USERS,), 0, ITEMS), jax.random.fold_in(streams_of[2], 1), 0, ITEMS - 1).astype(jnp.int32),
        "codebook": normal_values(streams_of[3], (LEVELS, K, D), 1.0, 6.0),
    }


def decode_items(codes, codebook):
    summed = jnp.zeros((codes.shape[1], codebook.shape[2]), jnp.float32)
    for level_idx in range(LEVELS):
        onehot = (codes[level_idx][:, None] == jnp.arange(K, dtype=jnp.int32)[None, :]).astype(jnp.bfloat16)
        summed = summed + jnp.dot(onehot, codebook[level_idx], preferred_element_type=jnp.float32)
    return summed


def split_three(grads):
    high = lax.optimization_barrier(grads.astype(jnp.bfloat16))
    rest = grads - high.astype(jnp.float32)
    middle = lax.optimization_barrier(rest.astype(jnp.bfloat16))
    low = (rest - middle.astype(jnp.float32)).astype(jnp.bfloat16)
    return (high, middle, low)


def codebook_terms(codes, grads):
    pieces = split_three(grads)
    levels_out = []
    for level_idx in range(LEVELS):
        onehot = (codes[level_idx][:, None] == jnp.arange(K, dtype=jnp.int32)[None, :]).astype(jnp.bfloat16)
        total = jnp.zeros((K, grads.shape[1]), jnp.float32)
        for piece in pieces:
            total = total + lax.dot_general(onehot, piece, (((0,), (0,)), ((), ())), preferred_element_type=jnp.float32)
        levels_out.append(total)
    return jnp.stack(levels_out)


def reference(user_emb, item_codes, targets, codebook):
    logit_scale = D ** -0.5
    item_vec = decode_items(item_codes, codebook).astype(jnp.bfloat16)
    columns = jnp.arange(ITEMS, dtype=jnp.int32)
    user_blocks = user_emb.reshape(N_USER, USER_BLK, D)
    target_blocks = targets.reshape(N_USER, USER_BLK)

    def one_block(carry, inputs):
        block_users, block_targets = inputs
        logits = jnp.dot(block_users, item_vec.T, preferred_element_type=jnp.float32) * logit_scale
        row_max = jnp.max(logits, axis=1)
        lse = row_max + jnp.log(jnp.sum(jnp.exp(logits - row_max[:, None]), axis=1))
        is_target = block_targets[:, None] == columns[None, :]
        pos_logit = jnp.sum(jnp.where(is_target, logits, 0.0), axis=1)
        dlogits = (jnp.exp(logits - lse[:, None]) - is_target.astype(jnp.float32)).astype(jnp.bfloat16)
        user_grad = jnp.dot(dlogits, item_vec, preferred_element_type=jnp.float32) * logit_scale
        carry = carry + jnp.dot(dlogits.T, block_users, preferred_element_type=jnp.float32) * logit_scale
        return carry, (user_grad, lse - pos_logit)

    grad_item, (user_grads, losses) = lax.scan(one_block, jnp.zeros((ITEMS, D), jnp.float32), (user_blocks, target_blocks))
    grad_codebook = codebook_terms(item_codes, grad_item)
    return user_grads.reshape(USERS, D), grad_codebook, jnp.mean(losses)
```

```python
import jax
import jax.numpy as jnp
from jax import lax
from jax.experimental import pallas as pl
from jax.experimental.pallas import tpu as pltpu
from jax.sharding import PartitionSpec as P

MESH = pl.DeviceIdType.MESH
NX, NY, NZ = 4, 8, 8
D = 256
K = 256
LEVELS = 3
OWN = 64
GROUP = 4
BLK = GROUP * OWN
ITEMS = 8192
CHUNK = 1024
STEPS = ITEMS // CHUNK
LANES = 128
SUBS = CHUNK // LANES
USERS = 32768
F32 = jnp.float32
BF16 = jnp.bfloat16


def dot(a, b):
    return jnp.dot(a, b, preferred_element_type=F32)


def dot_t(a, b):
    return lax.dot_general(a, b, (((1,), (1,)), ((), ())), preferred_element_type=F32)


def kernel(
    ue_hbm, codes_hbm, tg_hbm, cb_hbm, gu_ref, gc_ref, loss_ref,
    ub, us, cd, tg, slab, zb, yb, xb, tgb, cb, cbt, iota_k, col,
    oh, vt, lg, dl, mrun, srun, stat, lsec, tcol, pos,
    wacc, cbuf, dbuf, part, xr, ys, yr, zr, ay, fin,
    gus, gur, lv, ld, lx, ly, lz,
    loc, zs, zrs, tss, trs, uss, urs, yss, yrs, xss, xrs, sss, srs,
    ds, dr, xs1, xr1, ys1, yr1, zs1, zr1, ys2, yr2, xs2, xr2, ds2, dr2, gss, grs,
    lds, ldr, lxs, lxr, lys, lyr, lzs, lzr,
):
    u, i = lax.axis_index("user"), lax.axis_index("item")
    x, y = u // NY, lax.rem(u, NY)
    z, c = i // 2, lax.rem(i, 2)
    r = lax.rem(i, GROUP)
    sg = 1 - 2 * lax.rem(z, 2)

    def dev(x_, y_, z_, c_):
        return (x_ * NY + y_, z_ * 2 + c_)

    def xpeer(d):
        return lax.rem(x + d, NX)

    def ypeer(d):
        return lax.rem(y + d, NY)

    def zpeer(d):
        return lax.rem(z + d + NZ, NZ)

    zn = z + sg

    barrier = pltpu.get_barrier_semaphore()
    peers = [dev(xpeer(d), y, z, c) for d in range(1, NX)]
    peers += [dev(x, ypeer(d), z, c) for d in range(1, NY)]
    peers += [dev(x, y, zpeer(d), c) for d in range(1, NZ)]
    peers += [dev(x, y, z, 1 - c), dev(x, y, zn, 1 - c)]
    for peer in peers:
        pl.semaphore_signal(barrier, inc=1, device_id=peer, device_id_type=MESH)

    def send(src, dst, ss, rs, to):
        copy = pltpu.make_async_remote_copy(
            src_ref=src, dst_ref=dst, send_sem=ss, recv_sem=rs, device_id=to, device_id_type=MESH
        )
        copy.start()
        return copy

    own_rows = pl.ds(pl.multiple_of(r * OWN, OWN), OWN)
    loads = [
        pltpu.make_async_copy(codes_hbm, cd, loc.at[0]),
        pltpu.make_async_copy(tg_hbm, tg, loc.at[1]),
        pltpu.make_async_copy(ue_hbm, ub.at[own_rows, :], loc.at[2]),
        pltpu.make_async_copy(cb_hbm, cb, loc.at[3]),
    ]
    for load in loads:
        load.start()
    for load in loads[:3]:
        load.wait()

    own = cd[...].astype(F32)
    low = jnp.concatenate([own, jnp.zeros((LEVELS, OWN), F32)], axis=1)
    high = jnp.concatenate([jnp.zeros((LEVELS, OWN), F32), own], axis=1)
    none3 = jnp.zeros((3, LANES), F32)
    none2 = jnp.zeros((2, LANES), F32)
    slab[0] = jnp.concatenate([low, none3, none2], axis=0)
    slab[1] = jnp.concatenate([high, none3, none2], axis=0)
    slab[2] = jnp.concatenate([none3, low, none2], axis=0)
    slab[3] = jnp.concatenate([none3, high, none2], axis=0)
    t64 = tg[...]
    t128 = jnp.concatenate([t64, t64], axis=1)
    t256 = jnp.concatenate([t128, t128], axis=1)
    lane = lax.broadcasted_iota(jnp.int32, (8, BLK), 1)
    tgb[r] = jnp.where(lane // OWN == r, jnp.broadcast_to(t256, (8, BLK)), 0)

    pl.semaphore_wait(barrier, len(peers))

    zc = [
        send(slab.at[j], zb.at[j], zs.at[j], zrs.at[j], dev(x, y, zpeer(off), c))
        for j, off in ((1, -sg), (2, 2 * sg), (3, -3 * sg))
    ]
    mates = [dev(x, y, z, 1 - c), dev(x, y, zn, c), dev(x, y, zn, 1 - c)]
    mate_r = [lax.rem(r + 1, 2) + 2 * (r // 2), lax.rem(r + 2, 4), 3 - r]
    tc = [send(tgb.at[r], tgb.at[r], tss.at[k], trs.at[k], mates[k]) for k in range(3)]
    uc = [send(ub.at[own_rows, :], ub.at[own_rows, :], uss.at[k], urs.at[k], mates[k]) for k in range(3)]

    loads[3].wait()
    for l in range(LEVELS):
        cbt[:, l * K : (l + 1) * K] = cb[l * K : (l + 1) * K, :].astype(F32).T.astype(BF16)
    iota_k[...] = lax.broadcasted_iota(jnp.int32, (K, LANES), 0).astype(F32).astype(BF16)
    n = lax.broadcasted_iota(jnp.int32, (ITEMS // LANES, LANES), 0)
    k = lax.broadcasted_iota(jnp.int32, (ITEMS // LANES, LANES), 1)
    zj = (z - sg * (2 * (n % 2) + k // OWN) + NZ) % NZ
    uj = ((x + n // 16) % NX) * NY + (y + (n // 2) % NY) % NY
    col[...] = (zj * 2 + c) * 2048 + uj * OWN + k % OWN

    for cp in zc:
        cp.wait()
    yb[0] = (slab[0] + zb[1]) + (zb[2] + zb[3])
    yc = [send(yb.at[0], yb.at[NY - d], yss.at[d], yrs.at[d], dev(x, ypeer(d), z, c)) for d in range(1, NY)]
    for cp in tc + uc:
        cp.wait()
    us[...] = (ub[...].astype(F32) * (D**-0.5)).astype(BF16)
    tsum = (tgb[0] + tgb[1]) + (tgb[2] + tgb[3])
    tcol[...] = jnp.broadcast_to(tsum[0:1].astype(F32), (LANES, BLK)).T.astype(jnp.int32)
    mrun[...] = jnp.full((BLK, LANES), -1e30, F32)
    srun[...] = jnp.zeros((BLK, LANES), F32)
    pos[...] = jnp.zeros((BLK, LANES), F32)
    wacc[...] = jnp.zeros((K, BLK), F32)
    for cp in yc:
        cp.wait()
    xb[0] = yb[...].reshape(NY * 8, LANES).astype(BF16)
    xc = [send(xb.at[0], xb.at[NX - d], xss.at[d], xrs.at[d], dev(xpeer(d), y, z, c)) for d in range(1, NX)]

    def score(j, carry):
        base = pl.multiple_of(j * CHUNK, CHUNK)
        rows = xb[j // 2, pl.ds(pl.multiple_of(lax.rem(j, 2) * 32, 32), 32), :].astype(F32)
        for b in range(SUBS):
            for l in range(LEVELS):
                at = (b // 2) * 8 + (b % 2) * 3 + l
                row = jnp.broadcast_to(rows[at : at + 1, :], (16, LANES)).astype(BF16)
                hit = iota_k[...].reshape(K // 16, 16, LANES) == row[None]
                one = jnp.where(hit, jnp.ones((), BF16), jnp.zeros((), BF16))
                oh[l * K : (l + 1) * K, pl.ds(base + b * LANES, LANES)] = one.reshape(K, LANES)
        here = pl.ds(base, CHUNK)
        v = dot(cbt[...], oh[:, here]).astype(BF16)
        vt[:, here] = v
        lgt = dot(us[...], v)
        lg[:, here] = lgt
        m_old = mrun[...]
        m_new = m_old
        for b in range(SUBS):
            m_new = jnp.maximum(m_new, lgt[:, b * LANES : (b + 1) * LANES])
        s = srun[...] * jnp.exp(m_old - m_new)
        for b in range(SUBS):
            s = s + jnp.exp(lgt[:, b * LANES : (b + 1) * LANES] - m_new)
        mrun[...] = m_new
        srun[...] = s
        return carry

    lax.fori_loop(0, STEPS // NX, score, 0)
    for cp in xc:
        cp.wait()
    lax.fori_loop(STEPS // NX, STEPS, score, 0)

    mt = mrun[...].T
    st = srun[...].T
    m1 = jnp.max(mt, axis=0, keepdims=True)
    s1 = jnp.sum(st * jnp.exp(mt - m1), axis=0, keepdims=True)
    first = lax.broadcasted_iota(jnp.int32, (8, BLK), 0) == 0
    stat[r] = jnp.where(first, jnp.broadcast_to(m1, (8, BLK)), jnp.broadcast_to(s1, (8, BLK)))
    sc = [send(stat.at[r], stat.at[r], sss.at[k], srs.at[k], mates[k]) for k in range(3)]
    for cp in sc:
        cp.wait()
    ms = [stat[k][0:1] for k in range(GROUP)]
    top = jnp.maximum(jnp.maximum(ms[0], ms[1]), jnp.maximum(ms[2], ms[3]))
    tot = [stat[k][1:2] * jnp.exp(ms[k] - top) for k in range(GROUP)]
    lse = top + jnp.log((tot[0] + tot[1]) + (tot[2] + tot[3]))
    lsec[...] = jnp.broadcast_to(lse, (LANES, BLK)).T

    def grads(j, carry):
        base = pl.multiple_of(j * CHUNK, CHUNK)
        cols = col[pl.ds(pl.multiple_of(j * SUBS, SUBS), SUBS), :]
        for b in range(SUBS):
            here = pl.ds(base + b * LANES, LANES)
            lgt = lg[:, here]
            hit = tcol[...] == cols[b : b + 1, :]
            p = jnp.exp(lgt - lsec[...]) - jnp.where(hit, 1.0, 0.0)
            pos[...] += jnp.where(hit, lgt, 0.0)
            dl[:, here] = p.astype(BF16)
        here = pl.ds(base, CHUNK)
        wacc[...] += dot_t(oh[0:K, here], dl[:, here])
        return carry

    lax.fori_loop(0, STEPS, grads, 0)

    def level_out(l, w):
        hi = w.astype(BF16)
        rest = w - hi.astype(F32)
        mid = rest.astype(BF16)
        lo = (rest - mid.astype(F32)).astype(BF16)
        ubv = ub[...]
        out = (dot(hi, ubv) + dot(mid, ubv) + dot(lo, ubv)) * (D**-0.5)
        cbuf[l, 0] = out[:, :LANES]
        cbuf[l, 1] = out[:, LANES:]
        return send(cbuf.at[l, 1 - c], dbuf.at[l], ds.at[l], dr.at[l], dev(x, y, z, 1 - c))

    xrows = pl.ds(pl.multiple_of(x * 64, 64), 64)
    yrows = pl.ds(pl.multiple_of(y * 8, 8), 8)

    def x_send(l, cp):
        cp.wait()
        part[l] = cbuf[l, c] + dbuf[l]
        xr[l, x] = part[l, xrows, :]
        return [
            send(
                part.at[l, pl.ds(pl.multiple_of(xpeer(d) * 64, 64), 64), :], xr.at[l, x],
                xs1.at[l, d], xr1.at[l, d], dev(xpeer(d), y, z, c),
            )
            for d in range(1, NX)
        ]

    def l_send(val, buf, at, ss, rs, peer, count):
        buf[at] = val
        return [send(buf.at[at], buf.at[at], ss.at[d], rs.at[d], peer(d)) for d in range(1, count)]

    d0 = level_out(0, wacc[...])
    loss_part = 0.25 * jnp.sum(lse) - jnp.sum(pos[...])
    lv[...] = jnp.full((8, LANES), loss_part, F32)
    ldc = l_send(lv[...], ld, c, lds, ldr, lambda d: dev(x, y, z, 1 - c), 2)
    d1 = level_out(1, dot_t(oh[K : 2 * K, :], dl[...]))
    x0 = x_send(0, d0)
    for cp in ldc:
        cp.wait()
    lxc = l_send(ld[0] + ld[1], lx, x, lxs, lxr, lambda d: dev(xpeer(d), y, z, c), NX)
    d2 = level_out(2, dot_t(oh[2 * K : 3 * K, :], dl[...]))
    x1 = x_send(1, d1)
    gus[...] = dot_t(dl[...], vt[...]) * (D**-0.5)
    x2 = x_send(2, d2)
    guc = [
        send(
            gus.at[pl.ds(pl.multiple_of(mate_r[k] * OWN, OWN), OWN), :], gur.at[r],
            gss.at[k], grs.at[k], mates[k],
        )
        for k in range(3)
    ]
    gur[r] = gus[own_rows, :]

    def y_send(l, cps):
        for cp in cps:
            cp.wait()
        s = (xr[l, 0] + xr[l, 1]) + (xr[l, 2] + xr[l, 3])
        ys[l] = s
        yr[l, y] = ys[l, yrows, :]
        return [
            send(
                ys.at[l, pl.ds(pl.multiple_of(ypeer(d) * 8, 8), 8), :], yr.at[l, y],
                ys1.at[l, d], yr1.at[l, d], dev(x, ypeer(d), z, c),
            )
            for d in range(1, NY)
        ]

    def sum8(ref):
        return ((ref[0] + ref[1]) + (ref[2] + ref[3])) + ((ref[4] + ref[5]) + (ref[6] + ref[7]))

    def z_send(l, cps):
        for cp in cps:
            cp.wait()
        zr[l, z] = sum8(yr.at[l])
        return [
            send(zr.at[l, z], zr.at[l, z], zs1.at[l, d], zr1.at[l, d], dev(x, y, zpeer(d), c))
            for d in range(1, NZ)
        ]

    def y_back(l, cps):
        for cp in cps:
            cp.wait()
        ay[l, yrows, :] = sum8(zr.at[l])
        return [
            send(ay.at[l, yrows, :], ay.at[l, yrows, :], ys2.at[l, d], yr2.at[l, d], dev(x, ypeer(d), z, c))
            for d in range(1, NY)
        ]

    def x_back(l, cps):
        for cp in cps:
            cp.wait()
        fin[c, l, xrows, :] = ay[l]
        return [
            send(
                fin.at[c, l, xrows, :], fin.at[c, l, xrows, :],
                xs2.at[l, d], xr2.at[l, d], dev(xpeer(d), y, z, c),
            )
            for d in range(1, NX)
        ]

    def core_back(l, cps):
        for cp in cps:
            cp.wait()
        return send(fin.at[c, l], fin.at[c, l], ds2.at[l], dr2.at[l], dev(x, y, z, 1 - c))

    y0 = y_send(0, x0)
    for cp in lxc:
        cp.wait()
    lyc = l_send(
        (lx[0] + lx[1]) + (lx[2] + lx[3]), ly, y, lys, lyr, lambda d: dev(x, ypeer(d), z, c), NY
    )
    y1 = y_send(1, x1)
    y2 = y_send(2, x2)
    for cp in guc:
        cp.wait()
    gu_ref[...] = (gur[0] + gur[1]) + (gur[2] + gur[3])
    z0 = z_send(0, y0)
    for cp in lyc:
        cp.wait()
    lzc = l_send(sum8(ly), lz, z, lzs, lzr, lambda d: dev(x, y, zpeer(d), c), NZ)
    z1 = z_send(1, y1)
    z2 = z_send(2, y2)
    b0 = y_back(0, z0)
    for cp in lzc:
        cp.wait()
    loss_ref[...] = sum8(lz)[0:1, 0:1] * (1.0 / USERS)
    b1 = y_back(1, z1)
    b2 = y_back(2, z2)
    a0 = x_back(0, b0)
    a1 = x_back(1, b1)
    a2 = x_back(2, b2)
    e0 = core_back(0, a0)
    e1 = core_back(1, a1)
    e2 = core_back(2, a2)
    for l, cp in enumerate((e0, e1, e2)):
        cp.wait()
        gc_ref[l, :, 0:LANES] = fin[0, l]
        gc_ref[l, :, LANES:] = fin[1, l]


def shards(user_emb, item_codes, targets, codebook):
    vmem = pltpu.VMEM
    dma = pltpu.SemaphoreType.DMA
    scratch = [
        vmem((BLK, D), BF16), vmem((BLK, D), BF16), vmem((LEVELS, OWN), jnp.int32), vmem((1, OWN), jnp.int32),
        vmem((4, 8, LANES), F32), vmem((4, 8, LANES), F32), vmem((NY, 8, LANES), F32),
        vmem((NX, NY * 8, LANES), BF16), vmem((GROUP, 8, BLK), jnp.int32),
        vmem((LEVELS * K, D), BF16), vmem((D, LEVELS * K), BF16), vmem((K, LANES), BF16),
        vmem((ITEMS // LANES, LANES), jnp.int32),
        vmem((LEVELS * K, ITEMS), BF16), vmem((D, ITEMS), BF16), vmem((BLK, ITEMS), F32), vmem((BLK, ITEMS), BF16),
        vmem((BLK, LANES), F32), vmem((BLK, LANES), F32), vmem((GROUP, 8, BLK), F32), vmem((BLK, LANES), F32),
        vmem((BLK, LANES), jnp.int32), vmem((BLK, LANES), F32),
        vmem((K, BLK), F32), vmem((LEVELS, 2, K, LANES), F32), vmem((LEVELS, K, LANES), F32),
        vmem((LEVELS, K, LANES), F32), vmem((LEVELS, NX, 64, LANES), F32), vmem((LEVELS, 64, LANES), F32),
        vmem((LEVELS, NY, 8, LANES), F32), vmem((LEVELS, NZ, 8, LANES), F32), vmem((LEVELS, 64, LANES), F32),
        vmem((2, LEVELS, K, LANES), F32),
        vmem((BLK, D), F32), vmem((GROUP, OWN, D), F32), vmem((8, LANES), F32), vmem((2, 8, LANES), F32),
        vmem((NX, 8, LANES), F32), vmem((NY, 8, LANES), F32), vmem((NZ, 8, LANES), F32),
        dma((4,)), dma((4,)), dma((4,)), dma((3,)), dma((3,)), dma((3,)), dma((3,)),
        dma((NY,)), dma((NY,)), dma((NX,)), dma((NX,)), dma((3,)), dma((3,)),
        dma((LEVELS,)), dma((LEVELS,)), dma((LEVELS, NX)), dma((LEVELS, NX)), dma((LEVELS, NY)), dma((LEVELS, NY)),
        dma((LEVELS, NZ)), dma((LEVELS, NZ)), dma((LEVELS, NY)), dma((LEVELS, NY)), dma((LEVELS, NX)), dma((LEVELS, NX)),
        dma((LEVELS,)), dma((LEVELS,)), dma((3,)), dma((3,)),
        dma((2,)), dma((2,)), dma((NX,)), dma((NX,)), dma((NY,)), dma((NY,)), dma((NZ,)), dma((NZ,)),
    ]
    gu, gc, loss = pl.pallas_call(
        kernel,
        out_shape=(
            jax.ShapeDtypeStruct((OWN, D), F32),
            jax.ShapeDtypeStruct((LEVELS, K, D), F32),
            jax.ShapeDtypeStruct((1, 1), F32),
        ),
        in_specs=[pl.BlockSpec(memory_space=pl.ANY)] * 4,
        out_specs=[pl.BlockSpec(memory_space=vmem)] * 3,
        scratch_shapes=scratch,
        compiler_params=pltpu.CompilerParams(
            collective_id=0, has_side_effects=True, vmem_limit_bytes=56 * 2**20
        ),
        cost_estimate=pl.CostEstimate(flops=9 * 10**9, bytes_accessed=2 * 10**6, transcendentals=4 * 10**6),
    )(user_emb, item_codes, targets.reshape(1, OWN), codebook.reshape(LEVELS * K, D))
    return gu, gc, loss.reshape(())


def solution(mesh):
    return jax.shard_map(
        shards,
        mesh=mesh,
        in_specs=(P(("user", "item"), None), P(None, ("item", "user")), P(("user", "item")), P()),
        out_specs=(P(("user", "item"), None), P(), P()),
        check_vma=False,
    )
```

```python
import jax
import jax.numpy as jnp
from jax import lax
from jax.experimental import pallas as pl
from jax.experimental.pallas import tpu as pltpu
from jax.sharding import PartitionSpec as P

MESH = pl.DeviceIdType.MESH
NX, NY, NZ = 4, 8, 8
D = 256
K = 256
LEVELS = 3
OWN = 64
GROUP = 4
BLK = GROUP * OWN
ITEMS = 8192
CHUNK = 1024
STEPS = ITEMS // CHUNK
LANES = 128
SUBS = CHUNK // LANES
ROWS = 32
USERS = 32768
FAR = {4: (2, 1, 3), 8: (4, 3, 5, 2, 6, 1, 7)}
F32 = jnp.float32
BF16 = jnp.bfloat16


def dot(a, b):
    return jnp.dot(a, b, preferred_element_type=F32)


def dot_t(a, b):
    return lax.dot_general(a, b, (((1,), (1,)), ((), ())), preferred_element_type=F32)


def kernel(
    ue_hbm, codes_hbm, tg_hbm, cb_hbm, gu_ref, gc_ref, loss_ref,
    ub, us, cd, tg, slab, zb, yb, xb, tgb, cb, cbt, iota_k, col,
    oh, vt, lg, dl, mrun, srun, stat, lsec, tcol, pos,
    cbuf, dbuf, part, r1, s2, r2, r3, a4, fin,
    gus, gur, ld, lx, ly, lz,
    loc, zs, zrs, tss, trs, uss, urs, yss, yrs, xss, xrs, sss, srs,
    ds, dr, s1s, s1r, s2s, s2r, s3s, s3r, s4s, s4r, s5s, s5r, ds2, dr2, gss, grs,
    lds, ldr, lxs, lxr, lys, lyr, lzs, lzr,
):
    u, i = lax.axis_index("user"), lax.axis_index("item")
    x, y = u // NY, lax.rem(u, NY)
    z, c = i // 2, lax.rem(i, 2)
    r = lax.rem(i, GROUP)
    sg = 1 - 2 * lax.rem(z, 2)

    def dev(x_, y_, z_, c_):
        return (x_ * NY + y_, z_ * 2 + c_)

    def xpeer(d):
        return lax.rem(x + d, NX)

    def ypeer(d):
        return lax.rem(y + d, NY)

    def zpeer(d):
        return lax.rem(z + d + NZ, NZ)

    zn = z + sg

    barrier = pltpu.get_barrier_semaphore()
    peers = [dev(xpeer(d), y, z, c) for d in range(1, NX)]
    peers += [dev(x, ypeer(d), z, c) for d in range(1, NY)]
    peers += [dev(x, y, zpeer(d), c) for d in range(1, NZ)]
    peers += [dev(x, y, z, 1 - c), dev(x, y, zn, 1 - c)]
    for peer in peers:
        pl.semaphore_signal(barrier, inc=1, device_id=peer, device_id_type=MESH)

    sent = []

    def send(src, dst, ss, rs, to):
        copy = pltpu.make_async_remote_copy(
            src_ref=src, dst_ref=dst, send_sem=ss, recv_sem=rs, device_id=to, device_id_type=MESH
        )
        copy.start()
        sent.append(copy)
        return copy

    own_rows = pl.ds(pl.multiple_of(r * OWN, OWN), OWN)
    loads = [
        pltpu.make_async_copy(codes_hbm, cd, loc.at[0]),
        pltpu.make_async_copy(tg_hbm, tg, loc.at[1]),
        pltpu.make_async_copy(ue_hbm, ub.at[own_rows, :], loc.at[2]),
        pltpu.make_async_copy(cb_hbm, cb, loc.at[3]),
    ]
    for load in loads:
        load.start()
    for load in loads[:3]:
        load.wait()

    own = cd[...].astype(F32)
    low = jnp.concatenate([own, jnp.zeros((LEVELS, OWN), F32)], axis=1)
    high = jnp.concatenate([jnp.zeros((LEVELS, OWN), F32), own], axis=1)
    none3 = jnp.zeros((3, LANES), F32)
    none2 = jnp.zeros((2, LANES), F32)
    slab[0] = jnp.concatenate([low, none3, none2], axis=0)
    slab[1] = jnp.concatenate([high, none3, none2], axis=0)
    slab[2] = jnp.concatenate([none3, low, none2], axis=0)
    slab[3] = jnp.concatenate([none3, high, none2], axis=0)
    t64 = tg[...]
    t128 = jnp.concatenate([t64, t64], axis=1)
    t256 = jnp.concatenate([t128, t128], axis=1)
    lane = lax.broadcasted_iota(jnp.int32, (8, BLK), 1)
    tgb[r] = jnp.where(lane // OWN == r, jnp.broadcast_to(t256, (8, BLK)), 0)

    pl.semaphore_wait(barrier, len(peers))

    zc = [
        send(slab.at[j], zb.at[j], zs.at[j], zrs.at[j], dev(x, y, zpeer(off), c))
        for j, off in ((3, -3 * sg), (2, 2 * sg), (1, -sg))
    ]
    mates = [dev(x, y, z, 1 - c), dev(x, y, zn, c), dev(x, y, zn, 1 - c)]
    mate_r = [lax.rem(r + 1, 2) + 2 * (r // 2), lax.rem(r + 2, 4), 3 - r]
    tc = [send(tgb.at[r], tgb.at[r], tss.at[k], trs.at[k], mates[k]) for k in range(3)]
    uc = [send(ub.at[own_rows, :], ub.at[own_rows, :], uss.at[k], urs.at[k], mates[k]) for k in range(3)]

    loads[3].wait()
    for l in range(LEVELS):
        cbt[:, l * K : (l + 1) * K] = cb[l * K : (l + 1) * K, :].astype(F32).T.astype(BF16)
    iota_k[...] = lax.broadcasted_iota(jnp.int32, (K, LANES), 0).astype(F32).astype(BF16)
    n = lax.broadcasted_iota(jnp.int32, (ITEMS // LANES, LANES), 0)
    k = lax.broadcasted_iota(jnp.int32, (ITEMS // LANES, LANES), 1)
    zj = (z - sg * (2 * (n % 2) + k // OWN) + NZ) % NZ
    uj = ((x + n // 16) % NX) * NY + (y + (n // 2) % NY) % NY
    col[...] = (zj * 2 + c) * 2048 + uj * OWN + k % OWN

    for cp in zc:
        cp.wait_recv()
    yb[0] = (slab[0] + zb[1]) + (zb[2] + zb[3])
    yc = [send(yb.at[0], yb.at[NY - d], yss.at[d], yrs.at[d], dev(x, ypeer(d), z, c)) for d in FAR[NY]]
    for cp in tc + uc:
        cp.wait_recv()
    us[...] = (ub[...].astype(F32) * (D**-0.5)).astype(BF16)
    tsum = (tgb[0] + tgb[1]) + (tgb[2] + tgb[3])
    tcol[...] = jnp.broadcast_to(tsum[0:1].astype(F32), (LANES, BLK)).T.astype(jnp.int32)
    mrun[...] = jnp.full((BLK, LANES), -1e30, F32)
    srun[...] = jnp.zeros((BLK, LANES), F32)
    pos[...] = jnp.zeros((BLK, LANES), F32)
    for cp in yc:
        cp.wait_recv()
    xb[0] = yb[...].reshape(NY * 8, LANES).astype(BF16)
    xc = [send(xb.at[0], xb.at[NX - d], xss.at[d], xrs.at[d], dev(xpeer(d), y, z, c)) for d in FAR[NX]]

    def onehots(j):
        rows = xb[j // 2, (j % 2) * 32 : (j % 2) * 32 + 32, :].astype(F32)
        for b in range(SUBS):
            lanes = slice(j * CHUNK + b * LANES, j * CHUNK + (b + 1) * LANES)
            for l in range(LEVELS):
                at = (b // 2) * 8 + (b % 2) * 3 + l
                row = jnp.broadcast_to(rows[at : at + 1, :], (16, LANES)).astype(BF16)
                hit = iota_k[...].reshape(K // 16, 16, LANES) == row[None]
                one = jnp.where(hit, jnp.ones((), BF16), jnp.zeros((), BF16))
                oh[l * K : (l + 1) * K, lanes] = one.reshape(K, LANES)

    def span(j):
        return slice(j * CHUNK, (j + 1) * CHUNK)

    def stats(j):
        for top in range(0, BLK, ROWS):
            rows = slice(top, top + ROWS)
            tiles = [slice(j * CHUNK + b * LANES, j * CHUNK + (b + 1) * LANES) for b in range(SUBS)]
            m_old = mrun[rows]
            m_new = m_old
            for t in tiles:
                m_new = jnp.maximum(m_new, lg[rows, t])
            s = srun[rows] * jnp.exp(m_old - m_new)
            for t in tiles:
                s = s + jnp.exp(lg[rows, t] - m_new)
            mrun[rows] = m_new
            srun[rows] = s

    def score(first, last):
        onehots(first)
        for j in range(first, last + 2):
            if j < last:
                vt[:, span(j)] = dot(cbt[...], oh[:, span(j)]).astype(BF16)
            if j + 1 < last:
                onehots(j + 1)
            if first <= j - 1 < last:
                lg[:, span(j - 1)] = dot(us[...], vt[:, span(j - 1)])
            if first <= j - 2:
                stats(j - 2)

    score(0, STEPS // NX)
    for cp in xc:
        cp.wait_recv()
    score(STEPS // NX, STEPS)

    mt = mrun[...].T
    st = srun[...].T
    m1 = jnp.max(mt, axis=0, keepdims=True)
    s1 = jnp.sum(st * jnp.exp(mt - m1), axis=0, keepdims=True)
    first = lax.broadcasted_iota(jnp.int32, (8, BLK), 0) == 0
    stat[r] = jnp.where(first, jnp.broadcast_to(m1, (8, BLK)), jnp.broadcast_to(s1, (8, BLK)))
    sc = [send(stat.at[r], stat.at[r], sss.at[k], srs.at[k], mates[k]) for k in range(3)]
    for cp in sc:
        cp.wait_recv()
    ms = [stat[k][0:1] for k in range(GROUP)]
    top = jnp.maximum(jnp.maximum(ms[0], ms[1]), jnp.maximum(ms[2], ms[3]))
    tot = [stat[k][1:2] * jnp.exp(ms[k] - top) for k in range(GROUP)]
    lse = top + jnp.log((tot[0] + tot[1]) + (tot[2] + tot[3]))
    lsec[...] = jnp.broadcast_to(lse, (LANES, BLK)).T

    def dlogits(j):
        for top in range(0, BLK, ROWS):
            rows = slice(top, top + ROWS)
            t, e, found = tcol[rows], lsec[rows], pos[rows]
            for b in range(SUBS):
                lanes = slice(j * CHUNK + b * LANES, j * CHUNK + (b + 1) * LANES)
                v = lg[rows, lanes]
                hit = t == col[j * SUBS + b : j * SUBS + b + 1, :]
                p = jnp.exp(v - e)
                found = jnp.where(hit, v, found)
                dl[rows, lanes] = jnp.where(hit, p - 1.0, p).astype(BF16)
            pos[rows] = found

    dlogits(0)
    w = jnp.zeros((LEVELS * K, BLK), F32)
    for j in range(STEPS):
        w = w + dot_t(oh[:, span(j)], dl[:, span(j)])
        if j + 1 < STEPS:
            dlogits(j + 1)

    def level_out(l, w):
        hi = w.astype(BF16)
        rest = w - hi.astype(F32)
        mid = rest.astype(BF16)
        lo = (rest - mid.astype(F32)).astype(BF16)
        ubv = ub[...]
        out = (dot(hi, ubv) + dot(mid, ubv) + dot(lo, ubv)) * (D**-0.5)
        cbuf[l, 0] = out[:, :LANES]
        cbuf[l, 1] = out[:, LANES:]
        return send(cbuf.at[l, 1 - c], dbuf.at[l], ds.at[l], dr.at[l], dev(x, y, z, 1 - c))

    size = {"x": NX, "y": NY, "z": NZ}
    here = {"x": x, "y": y, "z": z}

    def along(a, d):
        if a == "x":
            return dev(xpeer(d), y, z, c)
        if a == "y":
            return dev(x, ypeer(d), z, c)
        return dev(x, y, zpeer(d), c)

    def block(at, rows):
        return pl.ds(pl.multiple_of(at * rows, 8), rows)

    def done(copies):
        for cp in copies:
            cp.wait_recv()

    def scatter(l, a, src, into, rows, ss, rs):
        n = size[a]
        into[l, block(here[a], rows), :] = src[l, block(here[a], rows), :]
        return [
            send(
                src.at[l, block(lax.rem(here[a] + d, n), rows), :], into.at[l, block(here[a], rows), :],
                ss.at[l, d], rs.at[l, d], along(a, d),
            )
            for d in FAR[n]
        ]

    def spread(buf, pre, a, rows, ss, rs, sem):
        at = buf.at[pre + (block(here[a], rows), slice(None))]
        return [send(at, at, ss.at[sem + (d,)], rs.at[sem + (d,)], along(a, d)) for d in FAR[size[a]]]

    def total(buf, pre, a, rows):
        parts = [buf[pre + (slice(k * rows, (k + 1) * rows), slice(None))] for k in range(size[a])]
        while len(parts) > 1:
            parts = [p + q for p, q in zip(parts[::2], parts[1::2])]
        return parts[0]

    ways = (("y", "x", "z"), ("z", "x", "y"), ("x", "y", "z"))

    def first(l, cp):
        cp.wait_recv()
        part[l] = cbuf[l, c] + dbuf[l]
        return scatter(l, ways[l][0], part, r1, K // size[ways[l][0]], s1s, s1r)

    def second(l, copies):
        done(copies)
        a, b, _ = ways[l]
        rows = K // size[a]
        s2[l, 0:rows, :] = total(r1, (l,), a, rows)
        return scatter(l, b, s2, r2, 8, s2s, s2r)

    def third(l, copies):
        done(copies)
        _, b, e = ways[l]
        r3[l, block(here[e], 8), :] = total(r2, (l,), b, 8)
        return spread(r3, (l,), e, 8, s3s, s3r, (l,))

    def fourth(l, copies):
        done(copies)
        _, b, e = ways[l]
        a4[l, block(here[b], 8), :] = total(r3, (l,), e, 8)
        return spread(a4, (l,), b, 8, s4s, s4r, (l,))

    def fifth(l, copies):
        done(copies)
        a = ways[l][0]
        rows = K // size[a]
        fin[c, l, block(here[a], rows), :] = a4[l, 0:rows, :]
        return spread(fin, (c, l), a, rows, s5s, s5r, (l,))

    def pass_on(l, at, rows, sem):
        there = fin.at[c, l, block(at, rows), :]
        return send(there, there, ds2.at[l, sem], dr2.at[l, sem], dev(x, y, z, 1 - c))

    def last(l, copies):
        a = ways[l][0]
        n = size[a]
        rows = K // n
        out = [pass_on(l, here[a], rows, 0)]
        for d, cp in sorted(zip(FAR[n], copies), key=lambda t: min(t[0], n - t[0])):
            cp.wait_recv()
            out.append(pass_on(l, lax.rem(here[a] + n - d, n), rows, d))
        return out

    def loss_over(a, val, buf, ss, rs):
        buf[block(here[a], 8), :] = val
        return spread(buf, (), a, 8, ss, rs, ())

    d0 = level_out(0, w[0:K])
    loss_part = 0.25 * jnp.sum(lse) - jnp.sum(pos[...])
    ld[c] = jnp.full((8, LANES), loss_part, F32)
    ldc = send(ld.at[c], ld.at[c], lds.at[0], ldr.at[0], dev(x, y, z, 1 - c))
    d1 = level_out(1, w[K : 2 * K])
    f0 = first(0, d0)
    d2 = level_out(2, w[2 * K :])
    f1 = first(1, d1)
    ldc.wait_recv()
    lxc = loss_over("x", ld[0] + ld[1], lx, lxs, lxr)
    gus[...] = dot_t(dl[...], vt[...]) * (D**-0.5)
    f2 = first(2, d2)
    g0 = second(0, f0)
    g1 = second(1, f1)
    done(lxc)
    lyc = loss_over("y", total(lx, (), "x", 8), ly, lys, lyr)
    g2 = second(2, f2)
    guc = [
        send(gus.at[block(mate_r[k], OWN), :], gur.at[r], gss.at[k], grs.at[k], mates[k]) for k in range(3)
    ]
    gur[r] = gus[own_rows, :]
    h0 = third(0, g0)
    h1 = third(1, g1)
    h2 = third(2, g2)
    done(lyc)
    lzc = loss_over("z", total(ly, (), "y", 8), lz, lzs, lzr)
    j0 = fourth(0, h0)
    j1 = fourth(1, h1)
    j2 = fourth(2, h2)
    done(lzc)
    loss_ref[...] = total(lz, (), "z", 8)[0:1, 0:1] * (1.0 / USERS)
    done(guc)
    gu_ref[...] = (gur[0] + gur[1]) + (gur[2] + gur[3])
    k0 = fifth(0, j0)
    k1 = fifth(1, j1)
    k2 = fifth(2, j2)
    e2 = last(2, k2)
    e0 = last(0, k0)
    e1 = last(1, k1)
    for l, copies in ((2, e2), (0, e0), (1, e1)):
        done(copies)
        gc_ref[l, :, 0:LANES] = fin[0, l]
        gc_ref[l, :, LANES:] = fin[1, l]
    for cp in sent:
        cp.wait_send()


def hand_over(gu_in, gc_in, loss_in, gu_ref, gc_ref, loss_ref):
    gu_ref[...] = gu_in[...]
    gc_ref[...] = gc_in[...]
    loss_ref[...] = loss_in[...]


def shards(user_emb, item_codes, targets, codebook):
    vmem = pltpu.VMEM
    dma = pltpu.SemaphoreType.DMA
    scratch = [
        vmem((BLK, D), BF16), vmem((BLK, D), BF16), vmem((LEVELS, OWN), jnp.int32), vmem((1, OWN), jnp.int32),
        vmem((4, 8, LANES), F32), vmem((4, 8, LANES), F32), vmem((NY, 8, LANES), F32),
        vmem((NX, NY * 8, LANES), BF16), vmem((GROUP, 8, BLK), jnp.int32),
        vmem((LEVELS * K, D), BF16), vmem((D, LEVELS * K), BF16), vmem((K, LANES), BF16),
        vmem((ITEMS // LANES, LANES), jnp.int32),
        vmem((LEVELS * K, ITEMS), BF16), vmem((D, ITEMS), BF16), vmem((BLK, ITEMS), F32), vmem((BLK, ITEMS), BF16),
        vmem((BLK, LANES), F32), vmem((BLK, LANES), F32), vmem((GROUP, 8, BLK), F32), vmem((BLK, LANES), F32),
        vmem((BLK, LANES), jnp.int32), vmem((BLK, LANES), F32),
        vmem((LEVELS, 2, K, LANES), F32), vmem((LEVELS, K, LANES), F32), vmem((LEVELS, K, LANES), F32),
        vmem((LEVELS, K, LANES), F32), vmem((LEVELS, 64, LANES), F32), vmem((LEVELS, 64, LANES), F32),
        vmem((LEVELS, 64, LANES), F32), vmem((LEVELS, 64, LANES), F32), vmem((2, LEVELS, K, LANES), F32),
        vmem((BLK, D), F32), vmem((GROUP, OWN, D), F32), vmem((2, 8, LANES), F32),
        vmem((NX * 8, LANES), F32), vmem((NY * 8, LANES), F32), vmem((NZ * 8, LANES), F32),
        dma((4,)), dma((4,)), dma((4,)), dma((3,)), dma((3,)), dma((3,)), dma((3,)),
        dma((NY,)), dma((NY,)), dma((NX,)), dma((NX,)), dma((3,)), dma((3,)),
        dma((LEVELS,)), dma((LEVELS,)), *[dma((LEVELS, 8)) for _ in range(10)],
        dma((LEVELS, 8)), dma((LEVELS, 8)), dma((3,)), dma((3,)),
        dma((2,)), dma((2,)), dma((NX,)), dma((NX,)), dma((NY,)), dma((NY,)), dma((NZ,)), dma((NZ,)),
    ]
    gu, gc, loss = pl.pallas_call(
        kernel,
        out_shape=(
            jax.ShapeDtypeStruct((OWN, D), F32),
            jax.ShapeDtypeStruct((LEVELS, K, D), F32),
            jax.ShapeDtypeStruct((1, 1), F32),
        ),
        in_specs=[pl.BlockSpec(memory_space=pl.ANY)] * 4,
        out_specs=[pl.BlockSpec(memory_space=vmem)] * 3,
        scratch_shapes=scratch,
        compiler_params=pltpu.CompilerParams(
            collective_id=0, has_side_effects=True, vmem_limit_bytes=56 * 2**20
        ),
        cost_estimate=pl.CostEstimate(flops=9 * 10**9, bytes_accessed=2 * 10**6, transcendentals=4 * 10**6),
    )(user_emb, item_codes, targets.reshape(1, OWN), codebook.reshape(LEVELS * K, D))
    gu, gc, loss = pl.pallas_call(
        hand_over,
        out_shape=tuple(jax.ShapeDtypeStruct(a.shape, F32) for a in (gu, gc, loss)),
        in_specs=[pl.BlockSpec(memory_space=vmem)] * 3,
        out_specs=[pl.BlockSpec(memory_space=vmem)] * 3,
    )(gu, gc, loss)
    return gu, gc, loss.reshape(())


def solution(mesh):
    return jax.shard_map(
        shards,
        mesh=mesh,
        in_specs=(P(("user", "item"), None), P(None, ("item", "user")), P(("user", "item")), P()),
        out_specs=(P(("user", "item"), None), P(), P()),
        check_vma=False,
    )
```

```python
import jax
import jax.numpy as jnp
from jax import lax
from jax.experimental import pallas as pl
from jax.experimental.pallas import tpu as pltpu
from jax.sharding import PartitionSpec as P

MESH = pl.DeviceIdType.MESH
NX, NY, NZ = 4, 8, 8
D = 256
K = 256
LEVELS = 3
OWN = 64
GROUP = 8
BLK = GROUP * OWN
ITEMS = 4096
CHUNK = 1024
STEPS = ITEMS // CHUNK
LANES = 128
SUBS = CHUNK // LANES
ROWS = 32
USERS = 32768
SLOT = (0, 1, 7, 2, 6, 3, 5, 4)
FAR = {4: (2, 1, 3), 8: (4, 3, 5, 2, 6, 1, 7)}
F32 = jnp.float32
BF16 = jnp.bfloat16


def dot(a, b):
    return jnp.dot(a, b, preferred_element_type=F32)


def dot_t(a, b):
    return lax.dot_general(a, b, (((1,), (1,)), ((), ())), preferred_element_type=F32)


def kernel(
    ue_hbm, codes_hbm, tg_hbm, cb_hbm, gu_ref, gc_ref, loss_ref,
    ub, us, cd, tg, slab, zb, yb, tgb, cb, cbt, iota_k, col,
    oh, vt, lg, dl, mrun, srun, stat, lsec, tcol, pos,
    cbuf, dbuf, part, r1, s2, r2, r3, a4, fin,
    gus, gud, gup, gur, guo, ld, lx, ly, lz,
    loc, zs, zrs, tss, trs, uss, urs, yss, yrs, sss, srs,
    ds, dr, s1s, s1r, s2s, s2r, s3s, s3r, s4s, s4r, s5s, s5r, ds2, dr2, gds, gdr, gss, grs, oss,
    lds, ldr, lxs, lxr, lys, lyr, lzs, lzr,
):
    u, i = lax.axis_index("user"), lax.axis_index("item")
    x, y = u // NY, lax.rem(u, NY)
    z, c = i // 2, lax.rem(i, 2)
    r = x * 2 + c

    def dev(x_, y_, z_, c_):
        return (x_ * NY + y_, z_ * 2 + c_)

    def xpeer(d):
        return lax.rem(x + d, NX)

    def ypeer(d):
        return lax.rem(y + d, NY)

    def zpeer(d):
        return lax.rem(z + d + NZ, NZ)

    barrier = pltpu.get_barrier_semaphore()
    peers = [dev(x, y, zpeer(d), c) for d in FAR[NZ]]
    peers += [dev(x, ypeer(d), z, c) for d in FAR[NY]]
    mates = [dev(xpeer(d), y, z, e) for d in FAR[NX] for e in (c, 1 - c)] + [dev(x, y, z, 1 - c)]
    peers += mates
    for peer in peers:
        pl.semaphore_signal(barrier, inc=1, device_id=peer, device_id_type=MESH)

    sent = []

    def send(src, dst, ss, rs, to):
        copy = pltpu.make_async_remote_copy(
            src_ref=src, dst_ref=dst, send_sem=ss, recv_sem=rs, device_id=to, device_id_type=MESH
        )
        copy.start()
        sent.append(copy)
        return copy

    own_rows = pl.ds(pl.multiple_of(r * OWN, OWN), OWN)
    loads = [
        pltpu.make_async_copy(codes_hbm, cd, loc.at[0]),
        pltpu.make_async_copy(tg_hbm, tg, loc.at[1]),
        pltpu.make_async_copy(ue_hbm, ub.at[own_rows, :], loc.at[2]),
        pltpu.make_async_copy(cb_hbm, cb, loc.at[3]),
    ]
    for load in loads:
        load.start()
    for load in loads[:3]:
        load.wait()

    own = cd[...].astype(F32)
    low = jnp.concatenate([own, jnp.zeros((LEVELS, OWN), F32)], axis=1)
    high = jnp.concatenate([jnp.zeros((LEVELS, OWN), F32), own], axis=1)
    none3 = jnp.zeros((3, LANES), F32)
    none2 = jnp.zeros((2, LANES), F32)
    slab[0] = jnp.concatenate([low, none3, none2], axis=0)
    slab[1] = jnp.concatenate([high, none3, none2], axis=0)
    slab[2] = jnp.concatenate([none3, low, none2], axis=0)
    slab[3] = jnp.concatenate([none3, high, none2], axis=0)
    t128 = jnp.concatenate([tg[...], tg[...]], axis=1)
    row8 = lax.broadcasted_iota(jnp.int32, (8, LANES), 0)
    lane = lax.broadcasted_iota(jnp.int32, (8, LANES), 1)
    mine = (row8 == x) & (lane // OWN == c)
    tgb[r] = jnp.where(mine, jnp.broadcast_to(t128, (8, LANES)), 0)

    pl.semaphore_wait(barrier, len(peers))

    zb[0] = slab[0]
    zc = [
        send(slab.at[(NZ - d) % 4], zb.at[NZ - d], zs.at[d], zrs.at[d], dev(x, y, zpeer(d), c)) for d in FAR[NZ]
    ]
    tc = [send(tgb.at[r], tgb.at[r], tss.at[k], trs.at[k], mates[k]) for k in range(GROUP - 1)]
    uc = [
        send(ub.at[own_rows, :], ub.at[own_rows, :], uss.at[k], urs.at[k], mates[k]) for k in range(GROUP - 1)
    ]

    loads[3].wait()
    for l in range(LEVELS):
        cbt[:, l * K : (l + 1) * K] = cb[l * K : (l + 1) * K, :].astype(F32).T.astype(BF16)
    iota_k[...] = lax.broadcasted_iota(jnp.int32, (K, LANES), 0).astype(F32).astype(BF16)
    n = lax.broadcasted_iota(jnp.int32, (ITEMS // LANES, LANES), 0)
    k = lax.broadcasted_iota(jnp.int32, (ITEMS // LANES, LANES), 1)
    step = n // 4
    dy = jnp.where(step % 2 == 1, (step + 1) // 2, (NY - step // 2) % NY)
    zj = (z + 2 * (n % 4) + k // OWN) % NZ
    col[...] = (zj * 2 + c) * 2048 + (x * NY + (y + dy) % NY) * OWN + k % OWN

    for cp in zc:
        cp.wait_recv()
    halves = [(zb[k] + zb[k + 1]) + (zb[k + 2] + zb[k + 3]) for k in (0, 4)]
    yb[0] = jnp.concatenate(halves, axis=0).astype(BF16)
    yc = {
        NY - d: send(yb.at[0], yb.at[SLOT.index(NY - d)], yss.at[d], yrs.at[d], dev(x, ypeer(d), z, c))
        for d in FAR[NY]
    }
    for cp in tc + uc:
        cp.wait_recv()
    us[...] = (ub[...].astype(F32) * (D**-0.5)).astype(BF16)
    tsum = ((tgb[0] + tgb[1]) + (tgb[2] + tgb[3])) + ((tgb[4] + tgb[5]) + (tgb[6] + tgb[7]))

    def column(row):
        return jnp.broadcast_to(row, (LANES, LANES)).T

    for q in range(BLK // LANES):
        tcol[q * LANES : (q + 1) * LANES, :] = column(tsum[q : q + 1].astype(F32)).astype(jnp.int32)
    mrun[...] = jnp.full((BLK, LANES), -1e30, F32)
    srun[...] = jnp.zeros((BLK, LANES), F32)
    pos[...] = jnp.zeros((BLK, LANES), F32)
    def onehots(j):
        rows = [yb[2 * j].astype(F32), yb[2 * j + 1].astype(F32)]
        for b in range(SUBS):
            lanes = slice(j * CHUNK + b * LANES, j * CHUNK + (b + 1) * LANES)
            for l in range(LEVELS):
                at = (b % 4 // 2) * 8 + (b % 2) * 3 + l
                row = jnp.broadcast_to(rows[b // 4][at : at + 1, :], (16, LANES)).astype(BF16)
                hit = iota_k[...].reshape(K // 16, 16, LANES) == row[None]
                one = jnp.where(hit, jnp.ones((), BF16), jnp.zeros((), BF16))
                oh[l * K : (l + 1) * K, lanes] = one.reshape(K, LANES)

    def span(j):
        return slice(j * CHUNK, (j + 1) * CHUNK)

    def stats(j):
        for top in range(0, BLK, ROWS):
            rows = slice(top, top + ROWS)
            tiles = [slice(j * CHUNK + b * LANES, j * CHUNK + (b + 1) * LANES) for b in range(SUBS)]
            m_old = mrun[rows]
            m_new = m_old
            for t in tiles:
                m_new = jnp.maximum(m_new, lg[rows, t])
            s = srun[rows] * jnp.exp(m_old - m_new)
            for t in tiles:
                s = s + jnp.exp(lg[rows, t] - m_new)
            mrun[rows] = m_new
            srun[rows] = s

    def score(first, last):
        onehots(first)
        for j in range(first, last + 2):
            if j < last:
                vt[:, span(j)] = dot(cbt[...], oh[:, span(j)]).astype(BF16)
            if j + 1 < last:
                onehots(j + 1)
            if first <= j - 1 < last:
                lg[:, span(j - 1)] = dot(us[...], vt[:, span(j - 1)])
            if first <= j - 2:
                stats(j - 2)

    for first in (0, STEPS // 2):
        for at in range(max(1, 2 * first), 2 * first + STEPS):
            yc[SLOT[at]].wait_recv()
        score(first, first + STEPS // 2)

    mt = mrun[...].T
    st = srun[...].T
    m1 = jnp.max(mt, axis=0, keepdims=True)
    s1 = jnp.sum(st * jnp.exp(mt - m1), axis=0, keepdims=True)
    quarters = [slice(q * LANES, (q + 1) * LANES) for q in range(BLK // LANES)]
    stat[r] = jnp.concatenate([m1[:, q] for q in quarters] + [s1[:, q] for q in quarters], axis=0)
    sc = [send(stat.at[r], stat.at[r], sss.at[k], srs.at[k], mates[k]) for k in range(GROUP - 1)]
    for cp in sc:
        cp.wait_recv()
    ms = [stat[k][0:4] for k in range(GROUP)]
    top = ms[0]
    for k in range(1, GROUP):
        top = jnp.maximum(top, ms[k])
    tot = [stat[k][4:8] * jnp.exp(ms[k] - top) for k in range(GROUP)]
    tot = ((tot[0] + tot[1]) + (tot[2] + tot[3])) + ((tot[4] + tot[5]) + (tot[6] + tot[7]))
    lse = top + jnp.log(tot)
    for q in range(BLK // LANES):
        lsec[q * LANES : (q + 1) * LANES, :] = column(lse[q : q + 1])
    def dlogits(j):
        for top in range(0, BLK, ROWS):
            rows = slice(top, top + ROWS)
            t, e, found = tcol[rows], lsec[rows], pos[rows]
            for b in range(SUBS):
                lanes = slice(j * CHUNK + b * LANES, j * CHUNK + (b + 1) * LANES)
                v = lg[rows, lanes]
                hit = t == col[j * SUBS + b : j * SUBS + b + 1, :]
                p = jnp.exp(v - e)
                found = jnp.where(hit, v, found)
                dl[rows, lanes] = jnp.where(hit, p - 1.0, p).astype(BF16)
            pos[rows] = found

    dlogits(0)
    w = jnp.zeros((LEVELS * K, BLK), F32)
    for j in range(STEPS):
        w = w + dot_t(oh[:, span(j)], dl[:, span(j)])
        if j + 1 < STEPS:
            dlogits(j + 1)

    def level_out(l, w):
        hi = w.astype(BF16)
        rest = w - hi.astype(F32)
        mid = rest.astype(BF16)
        lo = (rest - mid.astype(F32)).astype(BF16)
        ubv = ub[...]
        out = (dot(hi, ubv) + dot(mid, ubv) + dot(lo, ubv)) * (D**-0.5)
        cbuf[l, 0] = out[:, :LANES]
        cbuf[l, 1] = out[:, LANES:]
        return send(cbuf.at[l, 1 - c], dbuf.at[l], ds.at[l], dr.at[l], dev(x, y, z, 1 - c))

    size = {"x": NX, "y": NY, "z": NZ}
    here = {"x": x, "y": y, "z": z}

    def along(a, d):
        if a == "x":
            return dev(xpeer(d), y, z, c)
        if a == "y":
            return dev(x, ypeer(d), z, c)
        return dev(x, y, zpeer(d), c)

    def block(at, rows):
        return pl.ds(pl.multiple_of(at * rows, 8), rows)

    def done(copies):
        for cp in copies:
            cp.wait_recv()

    def scatter(l, a, src, into, rows, ss, rs):
        n = size[a]
        into[l, block(here[a], rows), :] = src[l, block(here[a], rows), :]
        return [
            send(
                src.at[l, block(lax.rem(here[a] + d, n), rows), :], into.at[l, block(here[a], rows), :],
                ss.at[l, d], rs.at[l, d], along(a, d),
            )
            for d in FAR[n]
        ]

    def spread(buf, pre, a, rows, ss, rs, sem):
        at = buf.at[pre + (block(here[a], rows), slice(None))]
        return [send(at, at, ss.at[sem + (d,)], rs.at[sem + (d,)], along(a, d)) for d in FAR[size[a]]]

    def total(buf, pre, a, rows):
        parts = [buf[pre + (slice(k * rows, (k + 1) * rows), slice(None))] for k in range(size[a])]
        while len(parts) > 1:
            parts = [p + q for p, q in zip(parts[::2], parts[1::2])]
        return parts[0]

    ways = (("y", "x", "z"), ("z", "x", "y"), ("x", "y", "z"))

    def first(l, cp):
        cp.wait_recv()
        part[l] = cbuf[l, c] + dbuf[l]
        return scatter(l, ways[l][0], part, r1, K // size[ways[l][0]], s1s, s1r)

    def second(l, copies):
        done(copies)
        a, b, _ = ways[l]
        rows = K // size[a]
        s2[l, 0:rows, :] = total(r1, (l,), a, rows)
        return scatter(l, b, s2, r2, 8, s2s, s2r)

    def third(l, copies):
        done(copies)
        _, b, e = ways[l]
        r3[l, block(here[e], 8), :] = total(r2, (l,), b, 8)
        return spread(r3, (l,), e, 8, s3s, s3r, (l,))

    def fourth(l, copies):
        done(copies)
        _, b, e = ways[l]
        a4[l, block(here[b], 8), :] = total(r3, (l,), e, 8)
        return spread(a4, (l,), b, 8, s4s, s4r, (l,))

    def fifth(l, copies):
        done(copies)
        a = ways[l][0]
        rows = K // size[a]
        fin[c, l, block(here[a], rows), :] = a4[l, 0:rows, :]
        return spread(fin, (c, l), a, rows, s5s, s5r, (l,))

    def pass_on(l, at, rows, sem):
        there = fin.at[c, l, block(at, rows), :]
        return send(there, there, ds2.at[l, sem], dr2.at[l, sem], dev(x, y, z, 1 - c))

    def last(l, copies):
        a = ways[l][0]
        n = size[a]
        rows = K // n
        out = [pass_on(l, here[a], rows, 0)]
        for d, cp in sorted(zip(FAR[n], copies), key=lambda t: min(t[0], n - t[0])):
            cp.wait_recv()
            out.append(pass_on(l, lax.rem(here[a] + n - d, n), rows, d))
        return out

    def loss_over(a, val, buf, ss, rs):
        buf[block(here[a], 8), :] = val
        return spread(buf, (), a, 8, ss, rs, ())

    d0 = level_out(0, w[0:K])
    loss_part = (1.0 / GROUP) * jnp.sum(lse) - jnp.sum(pos[...])
    ld[c] = jnp.full((8, LANES), loss_part, F32)
    ldc = send(ld.at[c], ld.at[c], lds.at[0], ldr.at[0], dev(x, y, z, 1 - c))
    d1 = level_out(1, w[K : 2 * K])
    f0 = first(0, d0)
    d2 = level_out(2, w[2 * K :])
    f1 = first(1, d1)
    ldc.wait_recv()
    lxc = loss_over("x", ld[0] + ld[1], lx, lxs, lxr)
    gu = dot_t(dl[...], vt[...]) * (D**-0.5)
    for k in range(GROUP):
        gus[k // 2, k % 2] = gu[k * OWN : (k + 1) * OWN]
    gdc = send(gus.at[:, 1 - c], gud, gds.at[0], gdr.at[0], dev(x, y, z, 1 - c))
    f2 = first(2, d2)
    g0 = second(0, f0)
    g1 = second(1, f1)
    done(lxc)
    lyc = loss_over("y", total(lx, (), "x", 8), ly, lys, lyr)
    g2 = second(2, f2)
    h0 = third(0, g0)
    h1 = third(1, g1)
    h2 = third(2, g2)
    done(lyc)
    lzc = loss_over("z", total(ly, (), "y", 8), lz, lzs, lzr)
    gdc.wait_recv()
    gup[...] = gus[:, c] + gud[...]
    gur[x] = gup[x]
    guc = [
        send(gup.at[xpeer(d)], gur.at[x], gss.at[d], grs.at[d], dev(xpeer(d), y, z, c)) for d in FAR[NX]
    ]
    j0 = fourth(0, h0)
    j1 = fourth(1, h1)
    j2 = fourth(2, h2)
    done(lzc)
    loss_ref[...] = total(lz, (), "z", 8)[0:1, 0:1] * (1.0 / USERS)
    done(guc)
    guo[...] = (gur[0] + gur[1]) + (gur[2] + gur[3])
    outs = [pltpu.make_async_copy(guo, gu_ref, oss.at[0, 0])]
    outs[0].start()
    k0 = fifth(0, j0)
    k1 = fifth(1, j1)
    k2 = fifth(2, j2)
    e2 = last(2, k2)
    e0 = last(0, k0)
    e1 = last(1, k1)
    for l, copies in ((2, e2), (0, e0), (1, e1)):
        done(copies)
        for half in range(2):
            out = pltpu.make_async_copy(
                fin.at[half, l], gc_ref.at[l, :, half * LANES : (half + 1) * LANES], oss.at[half, l + 1]
            )
            out.start()
            outs.append(out)
    for out in outs:
        out.wait()
    for cp in sent:
        cp.wait_send()


def hand_over(gu_in, gc_in, loss_in, gu_ref, gc_ref, loss_ref, gu, gc, ins, outs):
    pieces = [(gu_in, gu, gu_ref)] + [(gc_in.at[l], gc.at[l], gc_ref.at[l]) for l in range(LEVELS)]
    loads = [pltpu.make_async_copy(p[0], p[1], ins.at[k]) for k, p in enumerate(pieces)]
    stores = [pltpu.make_async_copy(p[1], p[2], outs.at[k]) for k, p in enumerate(pieces)]
    for load in loads:
        load.start()
    loss_ref[...] = loss_in[...]
    for load, store in zip(loads, stores):
        load.wait()
        store.start()
    for store in stores:
        store.wait()


def shards(user_emb, item_codes, targets, codebook):
    vmem = pltpu.VMEM
    dma = pltpu.SemaphoreType.DMA
    scratch = [
        vmem((BLK, D), BF16), vmem((BLK, D), BF16), vmem((LEVELS, OWN), jnp.int32), vmem((1, OWN), jnp.int32),
        vmem((4, 8, LANES), F32), vmem((NZ, 8, LANES), F32), vmem((NY, 16, LANES), BF16),
        vmem((GROUP, 8, LANES), jnp.int32),
        vmem((LEVELS * K, D), BF16), vmem((D, LEVELS * K), BF16), vmem((K, LANES), BF16),
        vmem((ITEMS // LANES, LANES), jnp.int32),
        vmem((LEVELS * K, ITEMS), BF16), vmem((D, ITEMS), BF16), vmem((BLK, ITEMS), F32), vmem((BLK, ITEMS), BF16),
        vmem((BLK, LANES), F32), vmem((BLK, LANES), F32), vmem((GROUP, 8, LANES), F32), vmem((BLK, LANES), F32),
        vmem((BLK, LANES), jnp.int32), vmem((BLK, LANES), F32),
        vmem((LEVELS, 2, K, LANES), F32), vmem((LEVELS, K, LANES), F32), vmem((LEVELS, K, LANES), F32),
        vmem((LEVELS, K, LANES), F32), vmem((LEVELS, 64, LANES), F32), vmem((LEVELS, 64, LANES), F32),
        vmem((LEVELS, 64, LANES), F32), vmem((LEVELS, 64, LANES), F32), vmem((2, LEVELS, K, LANES), F32),
        vmem((NX, 2, OWN, D), F32), vmem((NX, OWN, D), F32), vmem((NX, OWN, D), F32), vmem((NX, OWN, D), F32),
        vmem((OWN, D), F32), vmem((2, 8, LANES), F32),
        vmem((NX * 8, LANES), F32), vmem((NY * 8, LANES), F32), vmem((NZ * 8, LANES), F32),
        dma((4,)), dma((NZ,)), dma((NZ,)), dma((GROUP,)), dma((GROUP,)), dma((GROUP,)), dma((GROUP,)),
        dma((NY,)), dma((NY,)), dma((GROUP,)), dma((GROUP,)),
        dma((LEVELS,)), dma((LEVELS,)), *[dma((LEVELS, 8)) for _ in range(10)],
        dma((LEVELS, 8)), dma((LEVELS, 8)), dma((1,)), dma((1,)), dma((NX,)), dma((NX,)), dma((2, LEVELS + 1)),
        dma((2,)), dma((2,)), dma((NX,)), dma((NX,)), dma((NY,)), dma((NY,)), dma((NZ,)), dma((NZ,)),
    ]
    gu, gc, loss = pl.pallas_call(
        kernel,
        out_shape=(
            jax.ShapeDtypeStruct((OWN, D), F32),
            jax.ShapeDtypeStruct((LEVELS, K, D), F32),
            jax.ShapeDtypeStruct((1, 1), F32),
        ),
        in_specs=[pl.BlockSpec(memory_space=pl.ANY)] * 4,
        out_specs=[pl.BlockSpec(memory_space=m) for m in (pl.ANY, pl.ANY, vmem)],
        scratch_shapes=scratch,
        compiler_params=pltpu.CompilerParams(
            collective_id=0, has_side_effects=True, vmem_limit_bytes=56 * 2**20
        ),
        cost_estimate=pl.CostEstimate(flops=9 * 10**9, bytes_accessed=2 * 10**6, transcendentals=4 * 10**6),
    )(user_emb, item_codes, targets.reshape(1, OWN), codebook.reshape(LEVELS * K, D))
    gu, gc, loss = pl.pallas_call(
        hand_over,
        out_shape=tuple(jax.ShapeDtypeStruct(a.shape, F32) for a in (gu, gc, loss)),
        in_specs=[pl.BlockSpec(memory_space=m) for m in (pl.ANY, pl.ANY, vmem)],
        out_specs=[pl.BlockSpec(memory_space=m) for m in (pl.ANY, pl.ANY, vmem)],
        scratch_shapes=[vmem((OWN, D), F32), vmem((LEVELS, K, D), F32), dma((4,)), dma((4,))],
    )(gu, gc, loss)
    return gu, gc, loss.reshape(())


def solution(mesh):
    return jax.shard_map(
        shards,
        mesh=mesh,
        in_specs=(P(("user", "item"), None), P(None, ("item", "user")), P(("user", "item")), P()),
        out_specs=(P(("user", "item"), None), P(), P()),
        check_vma=False,
    )
```

```python
import jax
import jax.numpy as jnp
from jax import lax
from jax.experimental import pallas as pl
from jax.experimental.pallas import tpu as pltpu
from jax.sharding import PartitionSpec as P

MESH = pl.DeviceIdType.MESH
NX, NY, NZ = 4, 8, 8
D = 256
K = 256
LEVELS = 3
OWN = 64
GROUP = 8
BLK = GROUP * OWN
ITEMS = 4096
LANES = 128
SUBS = ITEMS // LANES
SCORE = (0, 4, 8, 16, 24, 32)
HALF = 16
GRADS = (0, 8, 16, 24, 32)
ROWS = 32
USERS = 32768
SLOT = (0, 1, 7, 2, 6, 3, 5, 4)
FAR = {4: (2, 1, 3), 8: (4, 3, 5, 2, 6, 1, 7)}
F32 = jnp.float32
BF16 = jnp.bfloat16


def dot(a, b):
    return jnp.dot(a, b, preferred_element_type=F32)


def dot_t(a, b):
    return lax.dot_general(a, b, (((1,), (1,)), ((), ())), preferred_element_type=F32)


def kernel(
    ue_hbm, codes_hbm, tg_hbm, cb_hbm, gu_ref, gc_ref, loss_ref,
    ub, us, cd, tg, slab, zb, yb, tgb, cb, cbt, iota_k, col,
    oh, vt, lg, dl, mrun, srun, stat, lsec, tcol, pos,
    cbuf, dbuf, part, r1, s2, r2, r3, a4, fin,
    gus, gud, gup, gur, ld, lx, ly, lz,
    loc, zs, zrs, tss, trs, uss, urs, yss, yrs, sss, srs,
    ds, dr, s1s, s1r, s2s, s2r, s3s, s3r, s4s, s4r, s5s, s5r, ds2, dr2, gds, gdr, gss, grs,
    lds, ldr, lxs, lxr, lys, lyr, lzs, lzr,
):
    u, i = lax.axis_index("user"), lax.axis_index("item")
    x, y = u // NY, lax.rem(u, NY)
    z, c = i // 2, lax.rem(i, 2)
    r = x * 2 + c

    def dev(x_, y_, z_, c_):
        return (x_ * NY + y_, z_ * 2 + c_)

    def xpeer(d):
        return lax.rem(x + d, NX)

    def ypeer(d):
        return lax.rem(y + d, NY)

    def zpeer(d):
        return lax.rem(z + d + NZ, NZ)

    barrier = pltpu.get_barrier_semaphore()
    peers = [dev(x, y, zpeer(d), c) for d in FAR[NZ]]
    peers += [dev(x, ypeer(d), z, c) for d in FAR[NY]]
    mates = [dev(xpeer(d), y, z, e) for d in FAR[NX] for e in (c, 1 - c)] + [dev(x, y, z, 1 - c)]
    peers += mates
    for peer in peers:
        pl.semaphore_signal(barrier, inc=1, device_id=peer, device_id_type=MESH)

    sent = []

    def send(src, dst, ss, rs, to):
        copy = pltpu.make_async_remote_copy(
            src_ref=src, dst_ref=dst, send_sem=ss, recv_sem=rs, device_id=to, device_id_type=MESH
        )
        copy.start()
        sent.append(copy)
        return copy

    own_rows = pl.ds(pl.multiple_of(r * OWN, OWN), OWN)
    loads = [
        pltpu.make_async_copy(codes_hbm, cd, loc.at[0]),
        pltpu.make_async_copy(tg_hbm, tg, loc.at[1]),
        pltpu.make_async_copy(ue_hbm, ub.at[own_rows, :], loc.at[2]),
        pltpu.make_async_copy(cb_hbm, cb, loc.at[3]),
    ]
    for load in loads:
        load.start()
    for load in loads[:3]:
        load.wait()

    own = cd[...].astype(F32)
    low = jnp.concatenate([own, jnp.zeros((LEVELS, OWN), F32)], axis=1)
    high = jnp.concatenate([jnp.zeros((LEVELS, OWN), F32), own], axis=1)
    none3 = jnp.zeros((3, LANES), F32)
    none2 = jnp.zeros((2, LANES), F32)
    slab[0] = jnp.concatenate([low, none3, none2], axis=0)
    slab[1] = jnp.concatenate([high, none3, none2], axis=0)
    slab[2] = jnp.concatenate([none3, low, none2], axis=0)
    slab[3] = jnp.concatenate([none3, high, none2], axis=0)
    t128 = jnp.concatenate([tg[...], tg[...]], axis=1)
    row8 = lax.broadcasted_iota(jnp.int32, (8, LANES), 0)
    lane = lax.broadcasted_iota(jnp.int32, (8, LANES), 1)
    mine = (row8 == x) & (lane // OWN == c)
    tgb[r] = jnp.where(mine, jnp.broadcast_to(t128, (8, LANES)), 0)

    pl.semaphore_wait(barrier, len(peers))

    zb[0] = slab[0]
    zc = [
        send(slab.at[(NZ - d) % 4], zb.at[NZ - d], zs.at[d], zrs.at[d], dev(x, y, zpeer(d), c)) for d in FAR[NZ]
    ]
    tc = [send(tgb.at[r], tgb.at[r], tss.at[k], trs.at[k], mates[k]) for k in range(GROUP - 1)]
    uc = [
        send(ub.at[own_rows, :], ub.at[own_rows, :], uss.at[k], urs.at[k], mates[k]) for k in range(GROUP - 1)
    ]

    loads[3].wait()
    for l in range(LEVELS):
        cbt[:, l * K : (l + 1) * K] = cb[l * K : (l + 1) * K, :].astype(F32).T.astype(BF16)
    iota_k[...] = lax.broadcasted_iota(jnp.int32, (K, LANES), 0).astype(F32).astype(BF16)
    n = lax.broadcasted_iota(jnp.int32, (ITEMS // LANES, LANES), 0)
    k = lax.broadcasted_iota(jnp.int32, (ITEMS // LANES, LANES), 1)
    step = n // 4
    dy = jnp.where(step % 2 == 1, (step + 1) // 2, (NY - step // 2) % NY)
    zj = (z + 2 * (n % 4) + k // OWN) % NZ
    col[...] = (zj * 2 + c) * 2048 + (x * NY + (y + dy) % NY) * OWN + k % OWN

    for cp in zc:
        cp.wait_recv()
    halves = [(zb[k] + zb[k + 1]) + (zb[k + 2] + zb[k + 3]) for k in (0, 4)]
    yb[0] = jnp.concatenate(halves, axis=0).astype(BF16)
    yc = {
        NY - d: send(yb.at[0], yb.at[SLOT.index(NY - d)], yss.at[d], yrs.at[d], dev(x, ypeer(d), z, c))
        for d in FAR[NY]
    }
    for cp in tc + uc:
        cp.wait_recv()
    us[...] = (ub[...].astype(F32) * (D**-0.5)).astype(BF16)
    tsum = ((tgb[0] + tgb[1]) + (tgb[2] + tgb[3])) + ((tgb[4] + tgb[5]) + (tgb[6] + tgb[7]))

    def column(row):
        return jnp.broadcast_to(row, (LANES, LANES)).T

    for q in range(BLK // LANES):
        tcol[q * LANES : (q + 1) * LANES, :] = column(tsum[q : q + 1].astype(F32)).astype(jnp.int32)
    mrun[...] = jnp.full((BLK, LANES), -1e30, F32)
    srun[...] = jnp.zeros((BLK, LANES), F32)
    pos[...] = jnp.zeros((BLK, LANES), F32)
    def tile(b):
        return slice(b * LANES, (b + 1) * LANES)

    def span(steps, j):
        return slice(steps[j] * LANES, steps[j + 1] * LANES)

    def onehots(j):
        for b in range(SCORE[j], SCORE[j + 1]):
            rows = yb[b // 4].astype(F32)
            for l in range(LEVELS):
                at = (b % 4 // 2) * 8 + (b % 2) * 3 + l
                row = jnp.broadcast_to(rows[at : at + 1, :], (16, LANES)).astype(BF16)
                hit = iota_k[...].reshape(K // 16, 16, LANES) == row[None]
                one = jnp.where(hit, jnp.ones((), BF16), jnp.zeros((), BF16))
                oh[l * K : (l + 1) * K, tile(b)] = one.reshape(K, LANES)

    def stats(j):
        blocks = range(SCORE[j], SCORE[j + 1])
        for top in range(0, BLK, ROWS):
            rows = slice(top, top + ROWS)
            m_old = mrun[rows]
            m_new = m_old
            for b in blocks:
                m_new = jnp.maximum(m_new, lg[rows, tile(b)])
            s = srun[rows] * jnp.exp(m_old - m_new)
            for b in blocks:
                s = s + jnp.exp(lg[rows, tile(b)] - m_new)
            mrun[rows] = m_new
            srun[rows] = s

    def arrived(first, last):
        for at in range(first, last):
            yc[SLOT[at]].wait_recv()

    steps = len(SCORE) - 1
    arrived(1, HALF // 4)
    onehots(0)
    for j in range(steps + 2):
        if j < steps:
            vt[:, span(SCORE, j)] = dot(cbt[...], oh[:, span(SCORE, j)]).astype(BF16)
        if j + 1 < steps:
            if SCORE[j + 1] == HALF:
                arrived(HALF // 4, NY)
            onehots(j + 1)
        if 1 <= j <= steps:
            lg[:, span(SCORE, j - 1)] = dot(us[...], vt[:, span(SCORE, j - 1)])
        if 2 <= j:
            stats(j - 2)

    mt = mrun[...].T
    st = srun[...].T
    m1 = jnp.max(mt, axis=0, keepdims=True)
    s1 = jnp.sum(st * jnp.exp(mt - m1), axis=0, keepdims=True)
    quarters = [slice(q * LANES, (q + 1) * LANES) for q in range(BLK // LANES)]
    stat[r] = jnp.concatenate([m1[:, q] for q in quarters] + [s1[:, q] for q in quarters], axis=0)
    sc = [send(stat.at[r], stat.at[r], sss.at[k], srs.at[k], mates[k]) for k in range(GROUP - 1)]
    for cp in sc:
        cp.wait_recv()
    ms = [stat[k][0:4] for k in range(GROUP)]
    top = ms[0]
    for k in range(1, GROUP):
        top = jnp.maximum(top, ms[k])
    tot = [stat[k][4:8] * jnp.exp(ms[k] - top) for k in range(GROUP)]
    tot = ((tot[0] + tot[1]) + (tot[2] + tot[3])) + ((tot[4] + tot[5]) + (tot[6] + tot[7]))
    lse = top + jnp.log(tot)
    for q in range(BLK // LANES):
        lsec[q * LANES : (q + 1) * LANES, :] = column(lse[q : q + 1])
    def dlogits(j):
        for top in range(0, BLK, ROWS):
            rows = slice(top, top + ROWS)
            t, e, found = tcol[rows], lsec[rows], pos[rows]
            for b in range(GRADS[j], GRADS[j + 1]):
                v = lg[rows, tile(b)]
                hit = t == col[b : b + 1, :]
                p = jnp.exp(v - e)
                found = jnp.where(hit, v, found)
                dl[rows, tile(b)] = jnp.where(hit, p - 1.0, p).astype(BF16)
            pos[rows] = found

    dlogits(0)
    w = jnp.zeros((LEVELS * K, BLK), F32)
    for j in range(len(GRADS) - 1):
        w = w + dot_t(oh[:, span(GRADS, j)], dl[:, span(GRADS, j)])
        if j + 2 < len(GRADS):
            dlogits(j + 1)

    def level_out(l, w):
        hi = w.astype(BF16)
        rest = w - hi.astype(F32)
        mid = rest.astype(BF16)
        lo = (rest - mid.astype(F32)).astype(BF16)
        ubv = ub[...]
        out = (dot(hi, ubv) + dot(mid, ubv) + dot(lo, ubv)) * (D**-0.5)
        cbuf[l, 0] = out[:, :LANES]
        cbuf[l, 1] = out[:, LANES:]
        return send(cbuf.at[l, 1 - c], dbuf.at[l], ds.at[l], dr.at[l], dev(x, y, z, 1 - c))

    size = {"x": NX, "y": NY, "z": NZ}
    here = {"x": x, "y": y, "z": z}

    def along(a, d):
        if a == "x":
            return dev(xpeer(d), y, z, c)
        if a == "y":
            return dev(x, ypeer(d), z, c)
        return dev(x, y, zpeer(d), c)

    def block(at, rows):
        return pl.ds(pl.multiple_of(at * rows, 8), rows)

    def done(copies):
        for cp in copies:
            cp.wait_recv()

    def scatter(l, a, src, into, rows, ss, rs):
        n = size[a]
        into[l, block(here[a], rows), :] = src[l, block(here[a], rows), :]
        return [
            send(
                src.at[l, block(lax.rem(here[a] + d, n), rows), :], into.at[l, block(here[a], rows), :],
                ss.at[l, d], rs.at[l, d], along(a, d),
            )
            for d in FAR[n]
        ]

    def spread(buf, pre, a, rows, ss, rs, sem):
        at = buf.at[pre + (block(here[a], rows), slice(None))]
        return [send(at, at, ss.at[sem + (d,)], rs.at[sem + (d,)], along(a, d)) for d in FAR[size[a]]]

    def total(buf, pre, a, rows):
        parts = [buf[pre + (slice(k * rows, (k + 1) * rows), slice(None))] for k in range(size[a])]
        while len(parts) > 1:
            parts = [p + q for p, q in zip(parts[::2], parts[1::2])]
        return parts[0]

    ways = (("y", "x", "z"), ("z", "x", "y"), ("x", "y", "z"))

    def first(l, cp):
        cp.wait_recv()
        part[l] = cbuf[l, c] + dbuf[l]
        return scatter(l, ways[l][0], part, r1, K // size[ways[l][0]], s1s, s1r)

    def second(l, copies):
        done(copies)
        a, b, _ = ways[l]
        rows = K // size[a]
        s2[l, 0:rows, :] = total(r1, (l,), a, rows)
        return scatter(l, b, s2, r2, 8, s2s, s2r)

    def third(l, copies):
        done(copies)
        _, b, e = ways[l]
        r3[l, block(here[e], 8), :] = total(r2, (l,), b, 8)
        return spread(r3, (l,), e, 8, s3s, s3r, (l,))

    def fourth(l, copies):
        done(copies)
        _, b, e = ways[l]
        a4[l, block(here[b], 8), :] = total(r3, (l,), e, 8)
        return spread(a4, (l,), b, 8, s4s, s4r, (l,))

    def fifth(l, copies):
        done(copies)
        a = ways[l][0]
        rows = K // size[a]
        fin[c, l, block(here[a], rows), :] = a4[l, 0:rows, :]
        return spread(fin, (c, l), a, rows, s5s, s5r, (l,))

    def pass_on(l, at, rows, sem):
        there = fin.at[c, l, block(at, rows), :]
        return send(there, there, ds2.at[l, sem], dr2.at[l, sem], dev(x, y, z, 1 - c))

    def last(l, copies):
        a = ways[l][0]
        n = size[a]
        rows = K // n
        out = [pass_on(l, here[a], rows, 0)]
        for d, cp in sorted(zip(FAR[n], copies), key=lambda t: min(t[0], n - t[0])):
            cp.wait_recv()
            out.append(pass_on(l, lax.rem(here[a] + n - d, n), rows, d))
        return out

    def loss_over(a, val, buf, ss, rs):
        buf[block(here[a], 8), :] = val
        return spread(buf, (), a, 8, ss, rs, ())

    d0 = level_out(0, w[0:K])
    own_lse = jnp.concatenate([lse * (1.0 / GROUP), jnp.zeros((4, LANES), F32)], axis=0)
    ld[c] = own_lse - jnp.sum(pos[...].reshape(BLK // 8, 8, LANES), axis=0)
    ldc = send(ld.at[c], ld.at[c], lds.at[0], ldr.at[0], dev(x, y, z, 1 - c))
    d1 = level_out(1, w[K : 2 * K])
    f0 = first(0, d0)
    d2 = level_out(2, w[2 * K :])
    f1 = first(1, d1)
    ldc.wait_recv()
    lxc = loss_over("x", ld[0] + ld[1], lx, lxs, lxr)
    f2 = first(2, d2)
    gu = dot_t(dl[...], vt[...]) * (D**-0.5)
    for k in range(GROUP):
        gus[k // 2, k % 2] = gu[k * OWN : (k + 1) * OWN]
    gdc = send(gus.at[:, 1 - c], gud, gds.at[0], gdr.at[0], dev(x, y, z, 1 - c))
    g0 = second(0, f0)
    g1 = second(1, f1)
    done(lxc)
    lyc = loss_over("y", total(lx, (), "x", 8), ly, lys, lyr)
    g2 = second(2, f2)
    h0 = third(0, g0)
    h1 = third(1, g1)
    h2 = third(2, g2)
    done(lyc)
    lzc = loss_over("z", total(ly, (), "y", 8), lz, lzs, lzr)
    gdc.wait_recv()
    gup[...] = gus[:, c] + gud[...]
    gur[x] = gup[x]
    guc = [
        send(gup.at[xpeer(d)], gur.at[x], gss.at[d], grs.at[d], dev(xpeer(d), y, z, c)) for d in FAR[NX]
    ]
    j0 = fourth(0, h0)
    j1 = fourth(1, h1)
    j2 = fourth(2, h2)
    done(lzc)
    loss_ref[...] = jnp.full((1, 1), jnp.sum(total(lz, (), "z", 8)) * (1.0 / USERS), F32)
    done(guc)
    gu_ref[...] = (gur[0] + gur[1]) + (gur[2] + gur[3])
    k0 = fifth(0, j0)
    k1 = fifth(1, j1)
    k2 = fifth(2, j2)
    e2 = last(2, k2)
    e0 = last(0, k0)
    e1 = last(1, k1)
    for l, copies in ((2, e2), (0, e0), (1, e1)):
        done(copies)
        gc_ref[l, :, :LANES] = fin[0, l]
        gc_ref[l, :, LANES:] = fin[1, l]
    for cp in sent:
        cp.wait_send()


def hand_over(gu_in, gc_in, loss_in, gu_ref, gc_ref, loss_ref):
    gu_ref[...] = gu_in[...]
    gc_ref[...] = gc_in[...]
    loss_ref[...] = loss_in[...]


def shards(user_emb, item_codes, targets, codebook):
    vmem = pltpu.VMEM
    dma = pltpu.SemaphoreType.DMA
    scratch = [
        vmem((BLK, D), BF16), vmem((BLK, D), BF16), vmem((LEVELS, OWN), jnp.int32), vmem((1, OWN), jnp.int32),
        vmem((4, 8, LANES), F32), vmem((NZ, 8, LANES), F32), vmem((NY, 16, LANES), BF16),
        vmem((GROUP, 8, LANES), jnp.int32),
        vmem((LEVELS * K, D), BF16), vmem((D, LEVELS * K), BF16), vmem((K, LANES), BF16),
        vmem((ITEMS // LANES, LANES), jnp.int32),
        vmem((LEVELS * K, ITEMS), BF16), vmem((D, ITEMS), BF16), vmem((BLK, ITEMS), F32), vmem((BLK, ITEMS), BF16),
        vmem((BLK, LANES), F32), vmem((BLK, LANES), F32), vmem((GROUP, 8, LANES), F32), vmem((BLK, LANES), F32),
        vmem((BLK, LANES), jnp.int32), vmem((BLK, LANES), F32),
        vmem((LEVELS, 2, K, LANES), F32), vmem((LEVELS, K, LANES), F32), vmem((LEVELS, K, LANES), F32),
        vmem((LEVELS, K, LANES), F32), vmem((LEVELS, 64, LANES), F32), vmem((LEVELS, 64, LANES), F32),
        vmem((LEVELS, 64, LANES), F32), vmem((LEVELS, 64, LANES), F32), vmem((2, LEVELS, K, LANES), F32),
        vmem((NX, 2, OWN, D), F32), vmem((NX, OWN, D), F32), vmem((NX, OWN, D), F32), vmem((NX, OWN, D), F32),
        vmem((2, 8, LANES), F32),
        vmem((NX * 8, LANES), F32), vmem((NY * 8, LANES), F32), vmem((NZ * 8, LANES), F32),
        dma((4,)), dma((NZ,)), dma((NZ,)), dma((GROUP,)), dma((GROUP,)), dma((GROUP,)), dma((GROUP,)),
        dma((NY,)), dma((NY,)), dma((GROUP,)), dma((GROUP,)),
        dma((LEVELS,)), dma((LEVELS,)), *[dma((LEVELS, 8)) for _ in range(10)],
        dma((LEVELS, 8)), dma((LEVELS, 8)), dma((1,)), dma((1,)), dma((NX,)), dma((NX,)),
        dma((2,)), dma((2,)), dma((NX,)), dma((NX,)), dma((NY,)), dma((NY,)), dma((NZ,)), dma((NZ,)),
    ]
    gu, gc, loss = pl.pallas_call(
        kernel,
        out_shape=tuple(jax.ShapeDtypeStruct(n, F32) for n in ((OWN, D), (LEVELS, K, D), (1, 1))),
        in_specs=[pl.BlockSpec(memory_space=pl.ANY)] * 4,
        out_specs=[pl.BlockSpec(memory_space=vmem)] * 3,
        scratch_shapes=scratch,
        compiler_params=pltpu.CompilerParams(
            collective_id=0, has_side_effects=True, vmem_limit_bytes=56 * 2**20
        ),
        cost_estimate=pl.CostEstimate(flops=9 * 10**9, bytes_accessed=2 * 10**6, transcendentals=4 * 10**6),
    )(user_emb, item_codes, targets.reshape(1, OWN), codebook.reshape(LEVELS * K, D))
    gu, gc, loss = pl.pallas_call(
        hand_over,
        out_shape=tuple(jax.ShapeDtypeStruct(n, F32) for n in ((OWN, D), (LEVELS, K, D), (1, 1))),
        in_specs=[pl.BlockSpec(memory_space=vmem)] * 3,
        out_specs=[pl.BlockSpec(memory_space=vmem)] * 3,
    )(gu, gc, loss)
    return gu, gc, loss.reshape(())


def solution(mesh):
    return jax.shard_map(
        shards,
        mesh=mesh,
        in_specs=(P(("user", "item"), None), P(None, ("item", "user")), P(("user", "item")), P()),
        out_specs=(P(("user", "item"), None), P(), P()),
        check_vma=False,
    )
```

```python
import jax
import jax.numpy as jnp
from jax import lax
from jax.experimental import pallas as pl
from jax.experimental.pallas import tpu as pltpu
from jax.sharding import PartitionSpec as P

MESH = pl.DeviceIdType.MESH
NX, NY, NZ = 4, 8, 8
D = 256
K = 256
LEVELS = 3
OWN = 64
GROUP = 8
BLK = GROUP * OWN
ITEMS = 4096
LANES = 128
SUBS = ITEMS // LANES
SCORE = (0, 4, 8, 16, 24, 32)
HALF = 16
GRADS = (0, 8, 16, 24, 32)
ROWS = 32
USERS = 32768
SLOT = (0, 1, 7, 2, 6, 3, 5, 4)
FAR = {4: (2, 1, 3), 8: (4, 3, 5, 2, 6, 1, 7)}
F32 = jnp.float32
BF16 = jnp.bfloat16


def dot(a, b):
    return jnp.dot(a, b, preferred_element_type=F32)


def dot_t(a, b):
    return lax.dot_general(a, b, (((1,), (1,)), ((), ())), preferred_element_type=F32)


def kernel(
    ue_hbm, codes_hbm, tg_hbm, cb_hbm, gu_ref, gc_ref, loss_ref,
    ub, us, cd, tg, slab, zb, yb, tgb, cb, cbt, iota_k, col,
    oh, vt, lg, dl, mrun, srun, stat, lsec, tcol, pos,
    cbuf, dbuf, part, r1, s2, r2, r3, a4, fin,
    gus, gud, gup, gur, ld, lx, ly, lz,
    loc, zs, tss, uss, yss, sss,
    ds, dr, s1s, s1r, s2s, s2r, s3s, s3r, s4s, s4r, s5s, s5r, ds2, dr2, gds, gdr, gss,
    lds, ldr, lxs, lxr, lys, lyr, lzs, lzr,
):
    u, i = lax.axis_index("user"), lax.axis_index("item")
    x, y = u // NY, lax.rem(u, NY)
    z, c = i // 2, lax.rem(i, 2)
    r = x * 2 + c

    def dev(x_, y_, z_, c_):
        return (x_ * NY + y_, z_ * 2 + c_)

    def xpeer(d):
        return lax.rem(x + d, NX)

    def ypeer(d):
        return lax.rem(y + d, NY)

    def zpeer(d):
        return lax.rem(z + d + NZ, NZ)

    barrier = pltpu.get_barrier_semaphore()
    peers = [dev(x, y, zpeer(d), c) for d in FAR[NZ]]
    peers += [dev(x, ypeer(d), z, c) for d in FAR[NY]]
    mates = [dev(xpeer(d), y, z, e) for d in FAR[NX] for e in (c, 1 - c)] + [dev(x, y, z, 1 - c)]
    peers += mates
    for peer in peers:
        pl.semaphore_signal(barrier, inc=1, device_id=peer, device_id_type=MESH)

    sent = []

    def take(size, sem):
        pltpu.make_async_copy(size, size, sem).wait()

    def push(src, dst, ss, rs, to):
        pltpu.make_async_remote_copy(
            src_ref=src, dst_ref=dst, send_sem=ss, recv_sem=rs, device_id=to, device_id_type=MESH
        ).start()

    def pushed(size, ss, rs):
        sent.append((size, ss))
        return lambda: take(size, rs)

    def send(src, dst, ss, rs, to):
        push(src, dst, ss, rs, to)
        return pushed(dst, ss, rs)

    own_rows = pl.ds(pl.multiple_of(r * OWN, OWN), OWN)
    loads = [
        pltpu.make_async_copy(codes_hbm, cd, loc.at[0]),
        pltpu.make_async_copy(tg_hbm, tg, loc.at[1]),
        pltpu.make_async_copy(ue_hbm, ub.at[own_rows, :], loc.at[2]),
        pltpu.make_async_copy(cb_hbm, cb, loc.at[3]),
    ]
    for load in loads:
        load.start()
    for load in loads[:3]:
        load.wait()

    own = cd[...].astype(F32)
    low = jnp.concatenate([own, jnp.zeros((LEVELS, OWN), F32)], axis=1)
    high = jnp.concatenate([jnp.zeros((LEVELS, OWN), F32), own], axis=1)
    none3 = jnp.zeros((3, LANES), F32)
    none2 = jnp.zeros((2, LANES), F32)
    slab[0] = jnp.concatenate([low, none3, none2], axis=0)
    slab[1] = jnp.concatenate([high, none3, none2], axis=0)
    slab[2] = jnp.concatenate([none3, low, none2], axis=0)
    slab[3] = jnp.concatenate([none3, high, none2], axis=0)
    t128 = jnp.concatenate([tg[...], tg[...]], axis=1)
    row8 = lax.broadcasted_iota(jnp.int32, (8, LANES), 0)
    lane = lax.broadcasted_iota(jnp.int32, (8, LANES), 1)
    mine = (row8 == x) & (lane // OWN == c)
    tgb[r] = jnp.where(mine, jnp.broadcast_to(t128, (8, LANES)), 0)

    pl.semaphore_wait(barrier, len(peers))

    zb[0] = slab[0]
    for d in FAR[NZ]:
        push(slab.at[(NZ - d) % 4], zb.at[NZ - d], zs.at[0], zs.at[1], dev(x, y, zpeer(d), c))
    zc = pushed(zb.at[1:NZ], zs.at[0], zs.at[1])
    for mate in mates:
        push(tgb.at[r], tgb.at[r], tss.at[0], tss.at[1], mate)
        push(ub.at[own_rows, :], ub.at[own_rows, :], uss.at[0], uss.at[1], mate)
    tc = pushed(tgb.at[1:GROUP], tss.at[0], tss.at[1])
    uc = pushed(ub.at[OWN:BLK, :], uss.at[0], uss.at[1])

    loads[3].wait()
    for l in range(LEVELS):
        cbt[:, l * K : (l + 1) * K] = cb[l * K : (l + 1) * K, :].astype(F32).T.astype(BF16)
    iota_k[...] = lax.broadcasted_iota(jnp.int32, (K, LANES), 0).astype(F32).astype(BF16)
    n = lax.broadcasted_iota(jnp.int32, (ITEMS // LANES, LANES), 0)
    k = lax.broadcasted_iota(jnp.int32, (ITEMS // LANES, LANES), 1)
    step = n // 4
    dy = jnp.where(step % 2 == 1, (step + 1) // 2, (NY - step // 2) % NY)
    zj = (z + 2 * (n % 4) + k // OWN) % NZ
    col[...] = (zj * 2 + c) * 2048 + (x * NY + (y + dy) % NY) * OWN + k % OWN

    zc()
    halves = [(zb[k] + zb[k + 1]) + (zb[k + 2] + zb[k + 3]) for k in (0, 4)]
    yb[0] = jnp.concatenate(halves, axis=0).astype(BF16)
    for d in FAR[NY]:
        at = SLOT.index(NY - d)
        push(yb.at[0], yb.at[at], yss.at[0], yss.at[1 + at // (HALF // 4)], dev(x, ypeer(d), z, c))
    sent.append((yb.at[1:NY], yss.at[0]))
    tc()
    uc()
    us[...] = (ub[...].astype(F32) * (D**-0.5)).astype(BF16)
    tsum = ((tgb[0] + tgb[1]) + (tgb[2] + tgb[3])) + ((tgb[4] + tgb[5]) + (tgb[6] + tgb[7]))

    def column(row):
        return jnp.broadcast_to(row, (LANES, LANES)).T

    for q in range(BLK // LANES):
        tcol[q * LANES : (q + 1) * LANES, :] = column(tsum[q : q + 1].astype(F32)).astype(jnp.int32)
    mrun[...] = jnp.full((BLK, LANES), -1e30, F32)
    srun[...] = jnp.zeros((BLK, LANES), F32)
    pos[...] = jnp.zeros((BLK, LANES), F32)
    def tile(b):
        return slice(b * LANES, (b + 1) * LANES)

    def span(steps, j):
        return slice(steps[j] * LANES, steps[j + 1] * LANES)

    def onehots(j):
        for b in range(SCORE[j], SCORE[j + 1]):
            rows = yb[b // 4].astype(F32)
            for l in range(LEVELS):
                at = (b % 4 // 2) * 8 + (b % 2) * 3 + l
                row = jnp.broadcast_to(rows[at : at + 1, :], (16, LANES)).astype(BF16)
                hit = iota_k[...].reshape(K // 16, 16, LANES) == row[None]
                one = jnp.where(hit, jnp.ones((), BF16), jnp.zeros((), BF16))
                oh[l * K : (l + 1) * K, tile(b)] = one.reshape(K, LANES)

    def stats(j):
        blocks = range(SCORE[j], SCORE[j + 1])
        for top in range(0, BLK, ROWS):
            rows = slice(top, top + ROWS)
            m_old = mrun[rows]
            m_new = m_old
            for b in blocks:
                m_new = jnp.maximum(m_new, lg[rows, tile(b)])
            s = srun[rows] * jnp.exp(m_old - m_new)
            for b in blocks:
                s = s + jnp.exp(lg[rows, tile(b)] - m_new)
            mrun[rows] = m_new
            srun[rows] = s

    steps = len(SCORE) - 1
    take(yb.at[1 : HALF // 4], yss.at[1])
    onehots(0)
    for j in range(steps + 2):
        if j < steps:
            vt[:, span(SCORE, j)] = dot(cbt[...], oh[:, span(SCORE, j)]).astype(BF16)
        if j + 1 < steps:
            if SCORE[j + 1] == HALF:
                take(yb.at[HALF // 4 : NY], yss.at[2])
            onehots(j + 1)
        if 1 <= j <= steps:
            lg[:, span(SCORE, j - 1)] = dot(us[...], vt[:, span(SCORE, j - 1)])
        if 2 <= j:
            stats(j - 2)

    mt = mrun[...].T
    st = srun[...].T
    m1 = jnp.max(mt, axis=0, keepdims=True)
    s1 = jnp.sum(st * jnp.exp(mt - m1), axis=0, keepdims=True)
    quarters = [slice(q * LANES, (q + 1) * LANES) for q in range(BLK // LANES)]
    stat[r] = jnp.concatenate([m1[:, q] for q in quarters] + [s1[:, q] for q in quarters], axis=0)
    for mate in mates:
        push(stat.at[r], stat.at[r], sss.at[0], sss.at[1], mate)
    pushed(stat.at[1:GROUP], sss.at[0], sss.at[1])()
    ms = [stat[k][0:4] for k in range(GROUP)]
    top = ms[0]
    for k in range(1, GROUP):
        top = jnp.maximum(top, ms[k])
    tot = [stat[k][4:8] * jnp.exp(ms[k] - top) for k in range(GROUP)]
    tot = ((tot[0] + tot[1]) + (tot[2] + tot[3])) + ((tot[4] + tot[5]) + (tot[6] + tot[7]))
    lse = top + jnp.log(tot)
    for q in range(BLK // LANES):
        lsec[q * LANES : (q + 1) * LANES, :] = column(lse[q : q + 1])
    def dlogits(j):
        for top in range(0, BLK, ROWS):
            rows = slice(top, top + ROWS)
            t, e, found = tcol[rows], lsec[rows], pos[rows]
            for b in range(GRADS[j], GRADS[j + 1]):
                v = lg[rows, tile(b)]
                hit = t == col[b : b + 1, :]
                p = jnp.exp(v - e)
                found = jnp.where(hit, v, found)
                dl[rows, tile(b)] = jnp.where(hit, p - 1.0, p).astype(BF16)
            pos[rows] = found

    dlogits(0)
    w = jnp.zeros((LEVELS * K, BLK), F32)
    for j in range(len(GRADS) - 1):
        w = w + dot_t(oh[:, span(GRADS, j)], dl[:, span(GRADS, j)])
        if j + 2 < len(GRADS):
            dlogits(j + 1)

    def level_out(l, w):
        hi = w.astype(BF16)
        rest = w - hi.astype(F32)
        mid = rest.astype(BF16)
        lo = (rest - mid.astype(F32)).astype(BF16)
        ubv = ub[...]
        out = (dot(hi, ubv) + dot(mid, ubv) + dot(lo, ubv)) * (D**-0.5)
        cbuf[l, 0] = out[:, :LANES]
        cbuf[l, 1] = out[:, LANES:]
        return send(cbuf.at[l, 1 - c], dbuf.at[l], ds.at[l], dr.at[l], dev(x, y, z, 1 - c))

    size = {"x": NX, "y": NY, "z": NZ}
    here = {"x": x, "y": y, "z": z}

    def along(a, d):
        if a == "x":
            return dev(xpeer(d), y, z, c)
        if a == "y":
            return dev(x, ypeer(d), z, c)
        return dev(x, y, zpeer(d), c)

    def block(at, rows):
        return pl.ds(pl.multiple_of(at * rows, 8), rows)

    def scatter(l, a, src, into, rows, ss, rs):
        n = size[a]
        into[l, block(here[a], rows), :] = src[l, block(here[a], rows), :]
        for d in FAR[n]:
            push(
                src.at[l, block(lax.rem(here[a] + d, n), rows), :], into.at[l, block(here[a], rows), :],
                ss.at[l], rs.at[l], along(a, d),
            )
        return pushed(into.at[l, rows : n * rows, :], ss.at[l], rs.at[l])

    def spread(buf, pre, a, rows, ss, rs):
        at = buf.at[pre + (block(here[a], rows), slice(None))]
        for d in FAR[size[a]]:
            push(at, at, ss, rs, along(a, d))
        return pushed(buf.at[pre + (slice(rows, size[a] * rows), slice(None))], ss, rs)

    def total(buf, pre, a, rows):
        parts = [buf[pre + (slice(k * rows, (k + 1) * rows), slice(None))] for k in range(size[a])]
        while len(parts) > 1:
            parts = [p + q for p, q in zip(parts[::2], parts[1::2])]
        return parts[0]

    ways = (("y", "x", "z"), ("z", "x", "y"), ("x", "y", "z"))

    def first(l, cp):
        cp()
        part[l] = cbuf[l, c] + dbuf[l]
        return scatter(l, ways[l][0], part, r1, K // size[ways[l][0]], s1s, s1r)

    def second(l, copies):
        copies()
        a, b, _ = ways[l]
        rows = K // size[a]
        s2[l, 0:rows, :] = total(r1, (l,), a, rows)
        return scatter(l, b, s2, r2, 8, s2s, s2r)

    def third(l, copies):
        copies()
        _, b, e = ways[l]
        r3[l, block(here[e], 8), :] = total(r2, (l,), b, 8)
        return spread(r3, (l,), e, 8, s3s.at[l], s3r.at[l])

    def fourth(l, copies):
        copies()
        _, b, e = ways[l]
        a4[l, block(here[b], 8), :] = total(r3, (l,), e, 8)
        return spread(a4, (l,), b, 8, s4s.at[l], s4r.at[l])

    def fifth(l, copies):
        copies()
        a = ways[l][0]
        rows = K // size[a]
        fin[c, l, block(here[a], rows), :] = a4[l, 0:rows, :]
        own = fin.at[c, l, block(here[a], rows), :]
        for d in FAR[size[a]]:
            push(own, own, s5s.at[l], s5r.at[l, d], along(a, d))
        sent.append((fin.at[c, l, rows:K, :], s5s.at[l]))

    def pass_on(l, at, rows):
        there = fin.at[c, l, block(at, rows), :]
        push(there, there, ds2.at[l], dr2.at[l], dev(x, y, z, 1 - c))

    def last(l):
        a = ways[l][0]
        n = size[a]
        rows = K // n
        pass_on(l, here[a], rows)
        for d in sorted(FAR[n], key=lambda d: min(d, n - d)):
            at = lax.rem(here[a] + n - d, n)
            take(fin.at[c, l, block(at, rows), :], s5r.at[l, d])
            pass_on(l, at, rows)
        return pushed(fin.at[1 - c, l], ds2.at[l], dr2.at[l])

    def loss_over(a, val, buf, ss, rs):
        buf[block(here[a], 8), :] = val
        return spread(buf, (), a, 8, ss.at[0], rs.at[0])

    d0 = level_out(0, w[0:K])
    own_lse = jnp.concatenate([lse * (1.0 / GROUP), jnp.zeros((4, LANES), F32)], axis=0)
    ld[c] = own_lse - jnp.sum(pos[...].reshape(BLK // 8, 8, LANES), axis=0)
    ldc = send(ld.at[c], ld.at[c], lds.at[0], ldr.at[0], dev(x, y, z, 1 - c))
    d1 = level_out(1, w[K : 2 * K])
    f0 = first(0, d0)
    d2 = level_out(2, w[2 * K :])
    f1 = first(1, d1)
    ldc()
    lxc = loss_over("x", ld[0] + ld[1], lx, lxs, lxr)
    f2 = first(2, d2)
    gu = dot_t(dl[...], vt[...]) * (D**-0.5)
    for k in range(GROUP):
        gus[k // 2, k % 2] = gu[k * OWN : (k + 1) * OWN]
    gdc = send(gus.at[:, 1 - c], gud, gds.at[0], gdr.at[0], dev(x, y, z, 1 - c))
    g0 = second(0, f0)
    g1 = second(1, f1)
    lxc()
    lyc = loss_over("y", total(lx, (), "x", 8), ly, lys, lyr)
    g2 = second(2, f2)
    h0 = third(0, g0)
    h1 = third(1, g1)
    h2 = third(2, g2)
    lyc()
    lzc = loss_over("z", total(ly, (), "y", 8), lz, lzs, lzr)
    gdc()
    gup[...] = gus[:, c] + gud[...]
    gur[x] = gup[x]
    for d in FAR[NX]:
        push(gup.at[xpeer(d)], gur.at[x], gss.at[0], gss.at[1], dev(xpeer(d), y, z, c))
    guc = pushed(gur.at[1:NX], gss.at[0], gss.at[1])
    j0 = fourth(0, h0)
    j1 = fourth(1, h1)
    j2 = fourth(2, h2)
    lzc()
    loss_ref[...] = jnp.full((1, 1), jnp.sum(total(lz, (), "z", 8)) * (1.0 / USERS), F32)
    guc()
    gu_ref[...] = (gur[0] + gur[1]) + (gur[2] + gur[3])
    fifth(0, j0)
    fifth(1, j1)
    fifth(2, j2)
    e2 = last(2)
    e0 = last(0)
    e1 = last(1)
    for l, copies in ((2, e2), (0, e0), (1, e1)):
        copies()
        gc_ref[l, :, :LANES] = fin[0, l]
        gc_ref[l, :, LANES:] = fin[1, l]
    for at, sem in sent:
        take(at, sem)


def hand_over(gu_in, gc_in, loss_in, gu_ref, gc_ref, loss_ref):
    gu_ref[...] = gu_in[...]
    gc_ref[...] = gc_in[...]
    loss_ref[...] = loss_in[...]


def shards(user_emb, item_codes, targets, codebook):
    vmem = pltpu.VMEM
    dma = pltpu.SemaphoreType.DMA
    scratch = [
        vmem((BLK, D), BF16), vmem((BLK, D), BF16), vmem((LEVELS, OWN), jnp.int32), vmem((1, OWN), jnp.int32),
        vmem((4, 8, LANES), F32), vmem((NZ, 8, LANES), F32), vmem((NY, 16, LANES), BF16),
        vmem((GROUP, 8, LANES), jnp.int32),
        vmem((LEVELS * K, D), BF16), vmem((D, LEVELS * K), BF16), vmem((K, LANES), BF16),
        vmem((ITEMS // LANES, LANES), jnp.int32),
        vmem((LEVELS * K, ITEMS), BF16), vmem((D, ITEMS), BF16), vmem((BLK, ITEMS), F32), vmem((BLK, ITEMS), BF16),
        vmem((BLK, LANES), F32), vmem((BLK, LANES), F32), vmem((GROUP, 8, LANES), F32), vmem((BLK, LANES), F32),
        vmem((BLK, LANES), jnp.int32), vmem((BLK, LANES), F32),
        vmem((LEVELS, 2, K, LANES), F32), vmem((LEVELS, K, LANES), F32), vmem((LEVELS, K, LANES), F32),
        vmem((LEVELS, K, LANES), F32), vmem((LEVELS, 64, LANES), F32), vmem((LEVELS, 64, LANES), F32),
        vmem((LEVELS, 64, LANES), F32), vmem((LEVELS, 64, LANES), F32), vmem((2, LEVELS, K, LANES), F32),
        vmem((NX, 2, OWN, D), F32), vmem((NX, OWN, D), F32), vmem((NX, OWN, D), F32), vmem((NX, OWN, D), F32),
        vmem((2, 8, LANES), F32),
        vmem((NX * 8, LANES), F32), vmem((NY * 8, LANES), F32), vmem((NZ * 8, LANES), F32),
        dma((4,)), dma((2,)), dma((2,)), dma((2,)), dma((3,)), dma((2,)),
        dma((LEVELS,)), dma((LEVELS,)), *[dma((LEVELS,)) for _ in range(9)], dma((LEVELS, NY)),
        dma((LEVELS,)), dma((LEVELS,)), dma((1,)), dma((1,)), dma((2,)), *[dma((1,)) for _ in range(8)],
    ]
    gu, gc, loss = pl.pallas_call(
        kernel,
        out_shape=tuple(jax.ShapeDtypeStruct(n, F32) for n in ((OWN, D), (LEVELS, K, D), (1, 1))),
        in_specs=[pl.BlockSpec(memory_space=pl.ANY)] * 4,
        out_specs=[pl.BlockSpec(memory_space=vmem)] * 3,
        scratch_shapes=scratch,
        compiler_params=pltpu.CompilerParams(
            collective_id=0, has_side_effects=True, vmem_limit_bytes=56 * 2**20
        ),
        cost_estimate=pl.CostEstimate(flops=9 * 10**9, bytes_accessed=2 * 10**6, transcendentals=4 * 10**6),
    )(user_emb, item_codes, targets.reshape(1, OWN), codebook.reshape(LEVELS * K, D))
    gu, gc, loss = pl.pallas_call(
        hand_over,
        out_shape=tuple(jax.ShapeDtypeStruct(n, F32) for n in ((OWN, D), (LEVELS, K, D), (1, 1))),
        in_specs=[pl.BlockSpec(memory_space=vmem)] * 3,
        out_specs=[pl.BlockSpec(memory_space=vmem)] * 3,
    )(gu, gc, loss)
    return gu, gc, loss.reshape(())


def solution(mesh):
    return jax.shard_map(
        shards,
        mesh=mesh,
        in_specs=(P(("user", "item"), None), P(None, ("item", "user")), P(("user", "item")), P()),
        out_specs=(P(("user", "item"), None), P(), P()),
        check_vma=False,
    )
```

```python
import jax
import jax.numpy as jnp
from jax import lax
from jax.experimental import pallas as pl
from jax.experimental.pallas import tpu as pltpu
from jax.sharding import PartitionSpec as P

MESH = pl.DeviceIdType.MESH
NX, NY, NZ = 4, 8, 8
D = 256
K = 256
LEVELS = 3
OWN = 64
GROUP = 8
BLK = GROUP * OWN
ITEMS = 4096
LANES = 128
SUBS = ITEMS // LANES
SCORE = (0, 4, 8, 16, 24, 32)
HALF = 16
GRADS = (0, 8, 16, 24, 32)
ROWS = 32
USERS = 32768
SLOT = (0, 1, 7, 2, 6, 3, 5, 4)
FAR = {4: (2, 1, 3), 8: (4, 3, 5, 2, 6, 1, 7)}
F32 = jnp.float32
BF16 = jnp.bfloat16


def dot(a, b):
    return jnp.dot(a, b, preferred_element_type=F32)


def dot_t(a, b):
    return lax.dot_general(a, b, (((1,), (1,)), ((), ())), preferred_element_type=F32)


def kernel(
    ue_hbm, codes_hbm, tg_hbm, cb_hbm, gu_ref, gc_ref, loss_ref,
    ub, us, cd, tg, slab, zb, yb, tgb, cb, cbt, iota_k, col,
    oh, vt, lg, dl, mrun, srun, stat, lsec, tcol, pos,
    cbuf, dbuf, part, r1, s2, r2, r3, a4, fin,
    gus, gud, gup, gur, guo, ld, lx, ly, lz,
    loc, zs, tss, uss, yss, sss,
    ds, dr, s1s, s1r, s2s, s2r, s3s, s3r, s4s, s4r, s5s, s5r, ds2, dr2, gds, gdr, gss, oss,
    lds, ldr, lxs, lxr, lys, lyr, lzs, lzr,
):
    u, i = lax.axis_index("user"), lax.axis_index("item")
    x, y = u // NY, lax.rem(u, NY)
    z, c = i // 2, lax.rem(i, 2)
    r = x * 2 + c

    def dev(x_, y_, z_, c_):
        return (x_ * NY + y_, z_ * 2 + c_)

    def xpeer(d):
        return lax.rem(x + d, NX)

    def ypeer(d):
        return lax.rem(y + d, NY)

    def zpeer(d):
        return lax.rem(z + d + NZ, NZ)

    barrier = pltpu.get_barrier_semaphore()
    peers = [dev(x, y, zpeer(d), c) for d in FAR[NZ]]
    peers += [dev(x, ypeer(d), z, c) for d in FAR[NY]]
    mates = [dev(xpeer(d), y, z, e) for d in FAR[NX] for e in (c, 1 - c)] + [dev(x, y, z, 1 - c)]
    peers += mates
    for peer in peers:
        pl.semaphore_signal(barrier, inc=1, device_id=peer, device_id_type=MESH)

    sent = []

    def take(size, sem):
        pltpu.make_async_copy(size, size, sem).wait()

    def push(src, dst, ss, rs, to):
        pltpu.make_async_remote_copy(
            src_ref=src, dst_ref=dst, send_sem=ss, recv_sem=rs, device_id=to, device_id_type=MESH
        ).start()

    def pushed(size, ss, rs):
        sent.append((size, ss))
        return lambda: take(size, rs)

    def send(src, dst, ss, rs, to):
        push(src, dst, ss, rs, to)
        return pushed(dst, ss, rs)

    own_rows = pl.ds(pl.multiple_of(r * OWN, OWN), OWN)
    loads = [
        pltpu.make_async_copy(codes_hbm, cd, loc.at[0]),
        pltpu.make_async_copy(tg_hbm, tg, loc.at[1]),
        pltpu.make_async_copy(ue_hbm, ub.at[own_rows, :], loc.at[2]),
        pltpu.make_async_copy(cb_hbm, cb, loc.at[3]),
    ]
    for load in loads:
        load.start()
    for load in loads[:3]:
        load.wait()

    own = cd[...].astype(F32)
    low = jnp.concatenate([own, jnp.zeros((LEVELS, OWN), F32)], axis=1)
    high = jnp.concatenate([jnp.zeros((LEVELS, OWN), F32), own], axis=1)
    none3 = jnp.zeros((3, LANES), F32)
    none2 = jnp.zeros((2, LANES), F32)
    slab[0] = jnp.concatenate([low, none3, none2], axis=0)
    slab[1] = jnp.concatenate([high, none3, none2], axis=0)
    slab[2] = jnp.concatenate([none3, low, none2], axis=0)
    slab[3] = jnp.concatenate([none3, high, none2], axis=0)
    t128 = jnp.concatenate([tg[...], tg[...]], axis=1)
    row8 = lax.broadcasted_iota(jnp.int32, (8, LANES), 0)
    lane = lax.broadcasted_iota(jnp.int32, (8, LANES), 1)
    mine = (row8 == x) & (lane // OWN == c)
    tgb[r] = jnp.where(mine, jnp.broadcast_to(t128, (8, LANES)), 0)

    pl.semaphore_wait(barrier, len(peers))

    zb[0] = slab[0]
    for d in FAR[NZ]:
        push(slab.at[(NZ - d) % 4], zb.at[NZ - d], zs.at[0], zs.at[1], dev(x, y, zpeer(d), c))
    zc = pushed(zb.at[1:NZ], zs.at[0], zs.at[1])
    for mate in mates:
        push(tgb.at[r], tgb.at[r], tss.at[0], tss.at[1], mate)
        push(ub.at[own_rows, :], ub.at[own_rows, :], uss.at[0], uss.at[1], mate)
    tc = pushed(tgb.at[1:GROUP], tss.at[0], tss.at[1])
    uc = pushed(ub.at[OWN:BLK, :], uss.at[0], uss.at[1])

    loads[3].wait()
    for l in range(LEVELS):
        cbt[:, l * K : (l + 1) * K] = cb[l * K : (l + 1) * K, :].astype(F32).T.astype(BF16)
    iota_k[...] = lax.broadcasted_iota(jnp.int32, (K, LANES), 0).astype(F32).astype(BF16)
    n = lax.broadcasted_iota(jnp.int32, (ITEMS // LANES, LANES), 0)
    k = lax.broadcasted_iota(jnp.int32, (ITEMS // LANES, LANES), 1)
    step = n // 4
    dy = jnp.where(step % 2 == 1, (step + 1) // 2, (NY - step // 2) % NY)
    zj = (z + 2 * (n % 4) + k // OWN) % NZ
    col[...] = (zj * 2 + c) * 2048 + (x * NY + (y + dy) % NY) * OWN + k % OWN

    zc()
    halves = [(zb[k] + zb[k + 1]) + (zb[k + 2] + zb[k + 3]) for k in (0, 4)]
    yb[0] = jnp.concatenate(halves, axis=0).astype(BF16)
    for d in FAR[NY]:
        at = SLOT.index(NY - d)
        push(yb.at[0], yb.at[at], yss.at[0], yss.at[1 + at // (HALF // 4)], dev(x, ypeer(d), z, c))
    sent.append((yb.at[1:NY], yss.at[0]))
    tc()
    uc()
    us[...] = (ub[...].astype(F32) * (D**-0.5)).astype(BF16)
    tsum = ((tgb[0] + tgb[1]) + (tgb[2] + tgb[3])) + ((tgb[4] + tgb[5]) + (tgb[6] + tgb[7]))

    def column(row):
        return jnp.broadcast_to(row, (LANES, LANES)).T

    for q in range(BLK // LANES):
        tcol[q * LANES : (q + 1) * LANES, :] = column(tsum[q : q + 1].astype(F32)).astype(jnp.int32)
    mrun[...] = jnp.full((BLK, LANES), -1e30, F32)
    srun[...] = jnp.zeros((BLK, LANES), F32)
    pos[...] = jnp.zeros((BLK, LANES), F32)
    def tile(b):
        return slice(b * LANES, (b + 1) * LANES)

    def span(steps, j):
        return slice(steps[j] * LANES, steps[j + 1] * LANES)

    def onehots(j):
        for b in range(SCORE[j], SCORE[j + 1]):
            rows = yb[b // 4].astype(F32)
            for l in range(LEVELS):
                at = (b % 4 // 2) * 8 + (b % 2) * 3 + l
                row = jnp.broadcast_to(rows[at : at + 1, :], (16, LANES)).astype(BF16)
                hit = iota_k[...].reshape(K // 16, 16, LANES) == row[None]
                one = jnp.where(hit, jnp.ones((), BF16), jnp.zeros((), BF16))
                oh[l * K : (l + 1) * K, tile(b)] = one.reshape(K, LANES)

    def stats(j):
        blocks = range(SCORE[j], SCORE[j + 1])
        for top in range(0, BLK, ROWS):
            rows = slice(top, top + ROWS)
            m_old = mrun[rows]
            m_new = m_old
            for b in blocks:
                m_new = jnp.maximum(m_new, lg[rows, tile(b)])
            s = srun[rows] * jnp.exp(m_old - m_new)
            for b in blocks:
                s = s + jnp.exp(lg[rows, tile(b)] - m_new)
            mrun[rows] = m_new
            srun[rows] = s

    steps = len(SCORE) - 1
    take(yb.at[1 : HALF // 4], yss.at[1])
    onehots(0)
    for j in range(steps + 2):
        if j < steps:
            vt[:, span(SCORE, j)] = dot(cbt[...], oh[:, span(SCORE, j)]).astype(BF16)
        if j + 1 < steps:
            if SCORE[j + 1] == HALF:
                take(yb.at[HALF // 4 : NY], yss.at[2])
            onehots(j + 1)
        if 1 <= j <= steps:
            lg[:, span(SCORE, j - 1)] = dot(us[...], vt[:, span(SCORE, j - 1)])
        if 2 <= j:
            stats(j - 2)

    mt = mrun[...].T
    st = srun[...].T
    m1 = jnp.max(mt, axis=0, keepdims=True)
    s1 = jnp.sum(st * jnp.exp(mt - m1), axis=0, keepdims=True)
    quarters = [slice(q * LANES, (q + 1) * LANES) for q in range(BLK // LANES)]
    stat[r] = jnp.concatenate([m1[:, q] for q in quarters] + [s1[:, q] for q in quarters], axis=0)
    for mate in mates:
        push(stat.at[r], stat.at[r], sss.at[0], sss.at[1], mate)
    pushed(stat.at[1:GROUP], sss.at[0], sss.at[1])()
    ms = [stat[k][0:4] for k in range(GROUP)]
    top = ms[0]
    for k in range(1, GROUP):
        top = jnp.maximum(top, ms[k])
    tot = [stat[k][4:8] * jnp.exp(ms[k] - top) for k in range(GROUP)]
    tot = ((tot[0] + tot[1]) + (tot[2] + tot[3])) + ((tot[4] + tot[5]) + (tot[6] + tot[7]))
    lse = top + jnp.log(tot)
    for q in range(BLK // LANES):
        lsec[q * LANES : (q + 1) * LANES, :] = column(lse[q : q + 1])
    def dlogits(j):
        for top in range(0, BLK, ROWS):
            rows = slice(top, top + ROWS)
            t, e, found = tcol[rows], lsec[rows], pos[rows]
            for b in range(GRADS[j], GRADS[j + 1]):
                v = lg[rows, tile(b)]
                hit = t == col[b : b + 1, :]
                p = jnp.exp(v - e)
                found = jnp.where(hit, v, found)
                dl[rows, tile(b)] = jnp.where(hit, p - 1.0, p).astype(BF16)
            pos[rows] = found

    dlogits(0)
    w = jnp.zeros((LEVELS * K, BLK), F32)
    for j in range(len(GRADS) - 1):
        w = w + dot_t(oh[:, span(GRADS, j)], dl[:, span(GRADS, j)])
        if j + 2 < len(GRADS):
            dlogits(j + 1)

    def level_out(l, w):
        hi = w.astype(BF16)
        rest = w - hi.astype(F32)
        mid = rest.astype(BF16)
        lo = (rest - mid.astype(F32)).astype(BF16)
        ubv = ub[...]
        out = (dot(hi, ubv) + dot(mid, ubv) + dot(lo, ubv)) * (D**-0.5)
        cbuf[l, 0] = out[:, :LANES]
        cbuf[l, 1] = out[:, LANES:]
        return send(cbuf.at[l, 1 - c], dbuf.at[l], ds.at[l], dr.at[l], dev(x, y, z, 1 - c))

    size = {"x": NX, "y": NY, "z": NZ}
    here = {"x": x, "y": y, "z": z}

    def along(a, d):
        if a == "x":
            return dev(xpeer(d), y, z, c)
        if a == "y":
            return dev(x, ypeer(d), z, c)
        return dev(x, y, zpeer(d), c)

    def block(at, rows):
        return pl.ds(pl.multiple_of(at * rows, 8), rows)

    def scatter(l, a, src, into, rows, ss, rs):
        n = size[a]
        into[l, block(here[a], rows), :] = src[l, block(here[a], rows), :]
        for d in FAR[n]:
            push(
                src.at[l, block(lax.rem(here[a] + d, n), rows), :], into.at[l, block(here[a], rows), :],
                ss.at[l], rs.at[l], along(a, d),
            )
        return pushed(into.at[l, rows : n * rows, :], ss.at[l], rs.at[l])

    def spread(buf, pre, a, rows, ss, rs):
        at = buf.at[pre + (block(here[a], rows), slice(None))]
        for d in FAR[size[a]]:
            push(at, at, ss, rs, along(a, d))
        return pushed(buf.at[pre + (slice(rows, size[a] * rows), slice(None))], ss, rs)

    def total(buf, pre, a, rows):
        parts = [buf[pre + (slice(k * rows, (k + 1) * rows), slice(None))] for k in range(size[a])]
        while len(parts) > 1:
            parts = [p + q for p, q in zip(parts[::2], parts[1::2])]
        return parts[0]

    ways = (("x", "z", "y"), ("y", "x", "z"), ("x", "y", "z"))

    def first(l, cp):
        cp()
        part[l] = cbuf[l, c] + dbuf[l]
        return scatter(l, ways[l][0], part, r1, K // size[ways[l][0]], s1s, s1r)

    def second(l, copies):
        copies()
        a, b, _ = ways[l]
        rows = K // size[a]
        s2[l, 0:rows, :] = total(r1, (l,), a, rows)
        return scatter(l, b, s2, r2, 8, s2s, s2r)

    def third(l, copies):
        copies()
        _, b, e = ways[l]
        r3[l, block(here[e], 8), :] = total(r2, (l,), b, 8)
        return spread(r3, (l,), e, 8, s3s.at[l], s3r.at[l])

    def fourth(l, copies):
        copies()
        _, b, e = ways[l]
        a4[l, block(here[b], 8), :] = total(r3, (l,), e, 8)
        return spread(a4, (l,), b, 8, s4s.at[l], s4r.at[l])

    def fifth(l, copies):
        copies()
        a = ways[l][0]
        rows = K // size[a]
        fin[c, l, block(here[a], rows), :] = a4[l, 0:rows, :]
        own = fin.at[c, l, block(here[a], rows), :]
        for d in FAR[size[a]]:
            push(own, own, s5s.at[l], s5r.at[l, d], along(a, d))
        sent.append((fin.at[c, l, rows:K, :], s5s.at[l]))

    def pass_on(l, at, rows):
        there = fin.at[c, l, block(at, rows), :]
        push(there, there, ds2.at[l], dr2.at[l], dev(x, y, z, 1 - c))

    def last(l):
        a = ways[l][0]
        n = size[a]
        rows = K // n
        pass_on(l, here[a], rows)
        for d in sorted(FAR[n], key=lambda d: min(d, n - d)):
            at = lax.rem(here[a] + n - d, n)
            take(fin.at[c, l, block(at, rows), :], s5r.at[l, d])
            pass_on(l, at, rows)
        return pushed(fin.at[1 - c, l], ds2.at[l], dr2.at[l])

    def loss_over(a, val, buf, ss, rs):
        buf[block(here[a], 8), :] = val
        return spread(buf, (), a, 8, ss.at[0], rs.at[0])

    d0 = level_out(0, w[0:K])
    own_lse = jnp.concatenate([lse * (1.0 / GROUP), jnp.zeros((4, LANES), F32)], axis=0)
    ld[c] = own_lse - jnp.sum(pos[...].reshape(BLK // 8, 8, LANES), axis=0)
    ldc = send(ld.at[c], ld.at[c], lds.at[0], ldr.at[0], dev(x, y, z, 1 - c))
    d1 = level_out(1, w[K : 2 * K])
    f0 = first(0, d0)
    d2 = level_out(2, w[2 * K :])
    f1 = first(1, d1)
    ldc()
    lxc = loss_over("x", ld[0] + ld[1], lx, lxs, lxr)
    f2 = first(2, d2)
    gu = dot_t(dl[...], vt[...]) * (D**-0.5)
    for k in range(GROUP):
        gus[k // 2, k % 2] = gu[k * OWN : (k + 1) * OWN]
    gdc = send(gus.at[:, 1 - c], gud, gds.at[0], gdr.at[0], dev(x, y, z, 1 - c))
    g0 = second(0, f0)
    g1 = second(1, f1)
    lxc()
    lyc = loss_over("y", total(lx, (), "x", 8), ly, lys, lyr)
    g2 = second(2, f2)
    h0 = third(0, g0)
    h1 = third(1, g1)
    h2 = third(2, g2)
    lyc()
    lzc = loss_over("z", total(ly, (), "y", 8), lz, lzs, lzr)
    gdc()
    gup[...] = gus[:, c] + gud[...]
    gur[x] = gup[x]
    for d in FAR[NX]:
        push(gup.at[xpeer(d)], gur.at[x], gss.at[0], gss.at[1], dev(xpeer(d), y, z, c))
    guc = pushed(gur.at[1:NX], gss.at[0], gss.at[1])
    j0 = fourth(0, h0)
    j1 = fourth(1, h1)
    j2 = fourth(2, h2)
    lzc()
    loss_ref[...] = jnp.full((1, 1), jnp.sum(total(lz, (), "z", 8)) * (1.0 / USERS), F32)
    guc()
    guo[...] = (gur[0] + gur[1]) + (gur[2] + gur[3])
    outs = [pltpu.make_async_copy(guo, gu_ref, oss.at[0, 0])]
    outs[0].start()
    fifth(0, j0)
    fifth(1, j1)
    fifth(2, j2)
    e2 = last(2)
    e0 = last(0)
    e1 = last(1)
    for l, copies in ((2, e2), (0, e0), (1, e1)):
        copies()
        for half in range(2):
            out = pltpu.make_async_copy(
                fin.at[half, l], gc_ref.at[l, :, half * LANES : (half + 1) * LANES], oss.at[half, l + 1]
            )
            out.start()
            outs.append(out)
    for out in outs:
        out.wait()
    for at, sem in sent:
        take(at, sem)


def hand_over(gu_in, gc_in, loss_in, gu_ref, gc_ref, loss_ref):
    gu_ref[...] = gu_in[...]
    gc_ref[...] = gc_in[...]
    loss_ref[...] = loss_in[...]


def shards(user_emb, item_codes, targets, codebook):
    vmem = pltpu.VMEM
    dma = pltpu.SemaphoreType.DMA
    scratch = [
        vmem((BLK, D), BF16), vmem((BLK, D), BF16), vmem((LEVELS, OWN), jnp.int32), vmem((1, OWN), jnp.int32),
        vmem((4, 8, LANES), F32), vmem((NZ, 8, LANES), F32), vmem((NY, 16, LANES), BF16),
        vmem((GROUP, 8, LANES), jnp.int32),
        vmem((LEVELS * K, D), BF16), vmem((D, LEVELS * K), BF16), vmem((K, LANES), BF16),
        vmem((ITEMS // LANES, LANES), jnp.int32),
        vmem((LEVELS * K, ITEMS), BF16), vmem((D, ITEMS), BF16), vmem((BLK, ITEMS), F32), vmem((BLK, ITEMS), BF16),
        vmem((BLK, LANES), F32), vmem((BLK, LANES), F32), vmem((GROUP, 8, LANES), F32), vmem((BLK, LANES), F32),
        vmem((BLK, LANES), jnp.int32), vmem((BLK, LANES), F32),
        vmem((LEVELS, 2, K, LANES), F32), vmem((LEVELS, K, LANES), F32), vmem((LEVELS, K, LANES), F32),
        vmem((LEVELS, K, LANES), F32), vmem((LEVELS, 64, LANES), F32), vmem((LEVELS, 64, LANES), F32),
        vmem((LEVELS, 64, LANES), F32), vmem((LEVELS, 64, LANES), F32), vmem((2, LEVELS, K, LANES), F32),
        vmem((NX, 2, OWN, D), F32), vmem((NX, OWN, D), F32), vmem((NX, OWN, D), F32), vmem((NX, OWN, D), F32),
        vmem((OWN, D), F32), vmem((2, 8, LANES), F32),
        vmem((NX * 8, LANES), F32), vmem((NY * 8, LANES), F32), vmem((NZ * 8, LANES), F32),
        dma((4,)), dma((2,)), dma((2,)), dma((2,)), dma((3,)), dma((2,)),
        dma((LEVELS,)), dma((LEVELS,)), *[dma((LEVELS,)) for _ in range(9)], dma((LEVELS, NY)),
        dma((LEVELS,)), dma((LEVELS,)), dma((1,)), dma((1,)), dma((2,)), dma((2, LEVELS + 1)), *[dma((1,)) for _ in range(8)],
    ]
    gu, gc, loss = pl.pallas_call(
        kernel,
        out_shape=tuple(jax.ShapeDtypeStruct(n, F32) for n in ((OWN, D), (LEVELS, K, D), (1, 1))),
        in_specs=[pl.BlockSpec(memory_space=pl.ANY)] * 4,
        out_specs=[pl.BlockSpec(memory_space=m) for m in (pl.ANY, pl.ANY, vmem)],
        scratch_shapes=scratch,
        compiler_params=pltpu.CompilerParams(
            collective_id=0, has_side_effects=True, vmem_limit_bytes=56 * 2**20
        ),
        cost_estimate=pl.CostEstimate(flops=9 * 10**9, bytes_accessed=2 * 10**6, transcendentals=4 * 10**6),
    )(user_emb, item_codes, targets.reshape(1, OWN), codebook.reshape(LEVELS * K, D))
    gu, gc, loss = pl.pallas_call(
        hand_over,
        out_shape=tuple(jax.ShapeDtypeStruct(n, F32) for n in ((OWN, D), (LEVELS, K, D), (1, 1))),
        in_specs=[pl.BlockSpec(memory_space=vmem)] * 3,
        out_specs=[pl.BlockSpec(memory_space=vmem)] * 3,
    )(gu, gc, loss)
    return gu, gc, loss.reshape(())


def solution(mesh):
    return jax.shard_map(
        shards,
        mesh=mesh,
        in_specs=(P(("user", "item"), None), P(None, ("item", "user")), P(("user", "item")), P()),
        out_specs=(P(("user", "item"), None), P(), P()),
        check_vma=False,
    )
```
